256 devices in a mesh: rows: 32 (over z_lo, y, core), rep: 8 (over x, z_hi).
Axes of the slice: x: 4, y: 4, z: 8 (z_hi: 2, z_lo: 4; z = z_hi * 4 + z_lo), core: 2. Of those that a mesh axis runs over, the one named last changes fastest.
Arguments:
- node_features: bfloat16 [65536, 256], P(('rows', 'rep')), may hold values from -6 to 6
- block_values: bfloat16 [256, 176, 128, 128], P(('rows', 'rep')), may hold values from -0.375 to 0.375
- block_rows: int32 [256, 176], P(('rows', 'rep')), may hold values from 0 to 15
- block_columns: int32 [256, 176], P(('rows', 'rep')), may hold values from 0 to 63
- block_used: int32 [256], P(('rows', 'rep')), may hold values from 23 to 176, as said below
- weight_self: bfloat16 [256, 128], replicated, may hold values from -0.375 to 0.375
- weight_message: bfloat16 [256, 128], replicated, may hold values from -0.375 to 0.375
- bias_hidden: float32 [128], replicated, may hold values from -3 to 3
- weight_output: bfloat16 [128, 256], replicated, may hold values from -0.5 to 0.5
- cotangent: bfloat16 [65536, 256], P(('rows', 'rep')), may hold values from -6 to 6
Outputs:
- updated: bfloat16 [65536, 256], P(('rows', 'rep'))
- grad_nodes: bfloat16 [65536, 256], P(('rows', 'rep'))
- grad_self: float32 [256, 128], replicated
- grad_message: float32 [256, 128], replicated
- grad_output: float32 [128, 256], replicated
- grad_bias: float32 [128], replicated
The draws below stay inside these ranges and needn't reach their ends.
Inputs may be any that keep to these rules, and one draw needn't show every extreme that they name: `block_used`: in every draw some group has all 176 slots in use.
All inputs are finite; a program needn't handle non-finite values.
Results may differ from the reference program's by a relative error of at most 0.022.
Values may be sent and summed in bfloat16 or wider, within the bound.
A program may use at most 64 MiB of HBM per device.

```python
import math
import jax
import jax.numpy as jnp
from jax import lax

FEAT = 256
HIDDEN_SIZE = 128
TILE = 128
NODE_DEV = 256
NBLK = 176
BROWS = 16
CTILES = 64
NODES = 65536
N_ROWS = 32
N_REP = 8
DEVICES = 256


def draw_block_used(key, part):
    key = jax.random.fold_in(key, 5)
    first, second = jax.random.split(key)
    counts = jax.random.randint(first, (DEVICES,), NBLK // 8 + 1, NBLK + 1)
    fullest = jax.random.randint(second, (), 0, DEVICES)
    return jnp.where(jnp.arange(DEVICES) == fullest, NBLK, counts).astype(jnp.int32)


def with_ends(values, rng, least, top_value):
    index_at = [jax.random.randint(jax.random.fold_in(rng, axis), (), 0, length) for axis, length in enumerate(values.shape)]
    widest = values.shape.index(max(values.shape))
    next_to = index_at[:widest] + [(index_at[widest] + 1) % values.shape[widest]] + index_at[widest + 1:]
    return values.at[tuple(index_at)].set(least).at[tuple(next_to)].set(top_value)


def steps_of(own_key, extent, shards, smallest, high):
    def one(dim, parts):
        steps = jax.random.uniform(jax.random.fold_in(jax.random.fold_in(own_key, 6), dim), (parts,), jnp.float32, smallest / len(shards), high / len(shards))
        return jnp.repeat(jnp.exp(steps), extent[dim] // parts).reshape((-1,) + (1,) * (len(extent) - dim - 1))

    loudness = one(*shards[0])
    for cut in shards[1:]:
        loudness = loudness * one(*cut)
    return loudness


def normal_values(own_key, shape, width, most, cuts=(), held_as=jnp.bfloat16):
    array = jax.random.normal(own_key, shape, jnp.float32) * width
    if len(cuts) > 0:
        array = steps_of(own_key, shape, cuts, -0.22, 0.18) * array
    return jnp.clip(array, min=-most, max=most).astype(held_as)


def setup_inputs(seed: int = 0) -> dict:
    streams_of = jax.random.split(jax.random.key(seed), 11)
    node_features = normal_values(streams_of[0], (NODES, FEAT), 1.0, 6.0, ((0, 256),))
    block_values = normal_values(streams_of[1], (DEVICES, NBLK, TILE, TILE), ((BROWS / (NBLK * TILE)) ** 0.5), 0.375, ((0, 256),))
    block_rows = with_ends(jax.random.randint(streams_of[2], (DEVICES, NBLK), 0, BROWS), jax.random.fold_in(streams_of[2], 1), 0, BROWS - 1).astype(jnp.int32)
    block_columns = with_ends(jax.random.randint(streams_of[3], (DEVICES, NBLK), 0, CTILES), jax.random.fold_in(streams_of[3], 1), 0, CTILES - 1).astype(jnp.int32)
    block_used = draw_block_used(jax.random.fold_in(streams_of[10], 71), 0)
    weight_self = normal_values(streams_of[5], (FEAT, HIDDEN_SIZE), FEAT ** -0.5, 0.375)
    weight_message = normal_values(streams_of[6], (FEAT, HIDDEN_SIZE), FEAT ** -0.5, 0.375)
    bias_hidden = normal_values(streams_of[7], (HIDDEN_SIZE,), 0.5, 3.0, (), jnp.float32)
    weight_output = normal_values(streams_of[8], (HIDDEN_SIZE, FEAT), HIDDEN_SIZE ** -0.5, 0.5)
    cotangent = normal_values(streams_of[9], (NODES, FEAT), 1.0, 6.0, ((0, 256),))
    return {"node_features": node_features, "block_values": block_values, "block_rows": block_rows, "block_columns": block_columns, "block_used": block_used, "weight_self": weight_self, "weight_message": weight_message, "bias_hidden": bias_hidden, "weight_output": weight_output, "cotangent": cotangent}


def reference(node_features, block_values, block_rows, block_columns, block_used, weight_self, weight_message, bias_hidden, weight_output, cotangent):
    highest = lax.Precision.HIGHEST
    feats4 = node_features.reshape(N_ROWS, N_REP, NODE_DEV, FEAT)
    slots = jnp.arange(NBLK, dtype=jnp.int32)

    def forward_group(totals, item):
        values, rows_of, cols_of, filled, group = item
        row_index = group // N_REP
        rep_index = group % N_REP
        column_space = lax.dynamic_index_in_dim(feats4, rep_index, 1, keepdims=False)
        column_space = column_space.reshape(CTILES, TILE, FEAT).astype(jnp.float32)
        picked = column_space[cols_of]
        product = jnp.einsum('bij,bjf->bif', values.astype(jnp.float32), picked, precision=highest)
        usable = (slots < filled).astype(jnp.float32)
        onehot = (rows_of[None, :] == jnp.arange(BROWS, dtype=jnp.int32)[:, None]).astype(jnp.float32) * usable[None, :]
        partial_value = jnp.einsum('rb,bif->rif', onehot, product, precision=highest).reshape(N_REP * NODE_DEV, FEAT)
        return (totals.at[row_index].add(partial_value), None)
    groups = jnp.arange(DEVICES, dtype=jnp.int32)
    start = jnp.zeros((N_ROWS, N_REP * NODE_DEV, FEAT), jnp.float32)
    totals, _ = lax.scan(forward_group, start, (block_values, block_rows, block_columns, block_used, groups))
    aggregated = totals.reshape(NODES, FEAT).astype(jnp.bfloat16)
    pre = jnp.dot(node_features, weight_self, preferred_element_type=jnp.float32) + jnp.dot(aggregated, weight_message, preferred_element_type=jnp.float32) + bias_hidden
    hidden = jax.nn.silu(pre).astype(jnp.bfloat16)
    updated = (node_features.astype(jnp.float32) + jnp.dot(hidden, weight_output, preferred_element_type=jnp.float32)).astype(jnp.bfloat16)
    hidden_grad = jnp.dot(cotangent, weight_output.T, preferred_element_type=jnp.float32)
    sigmoid_pre = jax.nn.sigmoid(pre)
    pre_grad = (hidden_grad * sigmoid_pre * (1.0 + pre * (1.0 - sigmoid_pre))).astype(jnp.bfloat16)
    factor = 1.0 / math.sqrt(NODES)
    grad_self = jnp.dot(node_features.T, pre_grad, preferred_element_type=jnp.float32) * factor
    grad_message = jnp.dot(aggregated.T, pre_grad, preferred_element_type=jnp.float32) * factor
    grad_output = jnp.dot(hidden.T, cotangent, preferred_element_type=jnp.float32) * factor
    grad_bias = lax.optimization_barrier(jnp.sum(pre_grad.astype(jnp.float32), axis=0)) * factor
    message_grad = jnp.dot(pre_grad, weight_message.T, preferred_element_type=jnp.float32).astype(jnp.bfloat16)
    grads3 = message_grad.reshape(N_ROWS, N_REP * NODE_DEV, FEAT)

    def backward_group(totals, item):
        values, rows_of, cols_of, filled, group = item
        row_index = group // N_REP
        rep_index = group % N_REP
        row_block = lax.dynamic_index_in_dim(grads3, row_index, 0, keepdims=False).reshape(BROWS, TILE, FEAT)
        picked = row_block[rows_of].astype(jnp.float32)
        product = jnp.einsum('bji,bjf->bif', values.astype(jnp.float32), picked, precision=highest)
        usable = (slots < filled).astype(jnp.float32)
        onehot = (cols_of[None, :] == jnp.arange(CTILES, dtype=jnp.int32)[:, None]).astype(jnp.float32) * usable[None, :]
        partial_value = jnp.einsum('cb,bif->cif', onehot, product, precision=highest).reshape(N_ROWS, NODE_DEV, FEAT)
        return (totals.at[:, rep_index].add(partial_value), None)
    start_back = jnp.zeros((N_ROWS, N_REP, NODE_DEV, FEAT), jnp.float32)
    back_totals, _ = lax.scan(backward_group, start_back, (block_values, block_rows, block_columns, block_used, groups))
    transposed = back_totals.reshape(NODES, FEAT)
    grad_nodes = (cotangent.astype(jnp.float32) + jnp.dot(pre_grad, weight_self.T, preferred_element_type=jnp.float32) + transposed).astype(jnp.bfloat16)
    return (updated, grad_nodes, grad_self, grad_message, grad_output, grad_bias)
```

```python
import functools
import math

import jax
import jax.numpy as jnp
from jax import lax
from jax.experimental import pallas as pl
from jax.experimental.pallas import tpu as pltpu
from jax.sharding import PartitionSpec as P

FEAT = 256
HID = 128
TILE = 128
NBLK = 176
NB_PAD = 256
BROWS = 16
CTILES = 64
ZERO_SLOT = NBLK
MESH = pl.DeviceIdType.MESH
F32 = jnp.float32
BF16 = jnp.bfloat16
UNROLL = 8
SELF_ROWS = 24
MSG_ROWS = 8


def dot(a, b, dims=((1,), (0,))):
    return lax.dot_general(a, b, (dims, ((), ())), preferred_element_type=F32)


def kernel(
    used_ref, x_ref, values_ref, brow_ref, bcol_ref, ws_ref, wm_ref, bias_ref, wo_ref, cot_ref,
    updated_ref, gnodes_ref, gself_ref, gmsg_ref, gout_ref, gbias_ref,
    vals, gath, xgath, runs, idx_v, idx_s, ident, base, hgrad,
    part_send, recv_a, recv_b, zsend, recv_z, pgt,
    t_send, recv_c, y_send, recv_y, z7_send, recv_z7,
    m_a, m_a_recv, m_a_in, m_a_rep, m_a_fin,
    m_b, m_b_recv, m_b_in, m_b_rep, m_b_fin,
    v_sem, i_sem, send_sems, p1z, p1y, p1c, xgz, xgy, xgc,
    r3a, r3b, r3z, r5x, r5z, r5f, r7c, r7y, r7z,
    aa_c, aa_in, aa_rep, aa_out, aa_f, ab_c, ab_in, ab_rep, ab_out, ab_f,
):
    row = lax.axis_index("rows")
    rep = lax.axis_index("rep")
    zl, y, c = row // 8, (row // 2) % 4, row % 2
    x, zh = rep // 2, rep % 2
    oc, ozh = 1 - c, 1 - zh

    def dev(zl_=None, y_=None, c_=None, x_=None, zh_=None):
        zl_ = zl if zl_ is None else zl_
        y_ = y if y_ is None else y_
        c_ = c if c_ is None else c_
        x_ = x if x_ is None else x_
        zh_ = zh if zh_ is None else zh_
        return {"rows": zl_ * 8 + y_ * 2 + c_, "rep": x_ * 2 + zh_}

    def around(i, d):
        return (i + d) % 4

    near = (1, 3, 2)
    sibling = dev(c_=oc)
    partner = dev(zh_=ozh)
    partners = [sibling, partner]
    for d in near:
        partners += [dev(y_=around(y, d)), dev(zl_=around(zl, d)), dev(x_=around(x, d))]
    barrier = pltpu.get_barrier_semaphore()
    for p in partners:
        pl.semaphore_signal(barrier, inc=1, device_id=p, device_id_type=MESH)

    load_values = pltpu.make_async_copy(values_ref.at[0], vals, v_sem)
    load_values.start()

    sent = []

    def send(src, dst, recv, to):
        copy = pltpu.make_async_remote_copy(
            src_ref=src, dst_ref=dst, send_sem=send_sems.at[len(sent)], recv_sem=recv,
            device_id=to, device_id_type=MESH,
        )
        copy.start()
        sent.append(copy)

    def arrived(dst, recv):
        pltpu.make_async_remote_copy(
            src_ref=dst, dst_ref=dst, send_sem=send_sems.at[0], recv_sem=recv,
            device_id=sibling, device_id_type=MESH,
        ).wait_recv()

    def shard(c_, y_, zl_):
        return gath.at[pl.ds((c_ * 16 + y_ * 4 + zl_) * 2, 2)]

    def xshards(c_, y_, zl_, n):
        return xgath.at[pl.ds(c_ * 16 + y_ * 4 + zl_, n)]

    feats = x_ref[...]
    mine = c * 16 + y * 4 + zl
    gath[pl.ds(mine * 2, 2)] = dot(feats, wm_ref[...]).astype(BF16).reshape(2, TILE, HID)
    xgath[mine] = feats
    pl.semaphore_wait(barrier, len(partners))
    own = shard(c, y, zl)
    for d in near:
        send(own, own, p1z.at[zl], dev(zl_=around(zl, d)))
    for d in near:
        send(own, own, p1y.at[y, zl], dev(y_=around(y, d)))
    send(own, own, p1c.at[y, zl], sibling)

    used = used_ref[0]
    idx_v[...] = jnp.zeros_like(idx_v)
    idx_v[0:1, 0:NBLK] = brow_ref[...]
    idx_v[1:2, 0:NBLK] = bcol_ref[...]
    lane = lax.broadcasted_iota(jnp.int32, (1, NB_PAD), 1)
    lanes = lax.broadcasted_iota(jnp.int32, (NB_PAD, NB_PAD), 1)
    usable = lane < used
    rows_of = idx_v[0:1, :]
    cols_of = idx_v[1:2, :]
    source = cols_of >> 1
    tile_of = (((source & 1) * 16 + ((source >> 1) & 3) * 4 + (source >> 3)) << 1) + (cols_of & 1)

    def listing(key, other):
        packed = (((key << 8) + lane) << 7) + other
        along = jnp.broadcast_to(packed, (NB_PAD, NB_PAD))
        down = along.T
        rank = jnp.sum((along < down).astype(jnp.int32), axis=1, keepdims=True)
        ordered = jnp.sum(jnp.where(rank == lanes, down, 0), axis=0, keepdims=True)
        keys = down >> 15
        upto = jnp.sum((keys <= lanes).astype(jnp.int32), axis=0, keepdims=True)
        below = jnp.sum((keys < lanes).astype(jnp.int32), axis=0, keepdims=True)
        return ordered, jnp.where(upto > below, upto - 1, ZERO_SLOT)

    order_f, end_f = listing(jnp.where(usable, rows_of, BROWS), tile_of)
    order_b, end_b = listing(jnp.where(usable, tile_of, CTILES), rows_of)
    idx_v[0:1, :] = order_f
    idx_v[1:2, :] = end_f
    idx_v[2:3, :] = order_b
    idx_v[3:4, :] = end_b
    load_index = pltpu.make_async_copy(idx_v, idx_s, i_sem)
    load_index.start()

    for d in near:
        zs = around(zl, d)
        arrived(shard(c, y, zs), p1z.at[zs])
        for e in near:
            send(shard(c, y, zs), shard(c, y, zs), p1y.at[y, zs], dev(y_=around(y, e)))
        send(shard(c, y, zs), shard(c, y, zs), p1c.at[y, zs], sibling)
    for d in near:
        send(xshards(c, y, zl, 1), xshards(c, y, zl, 1), xgz.at[zl], dev(zl_=around(zl, d)))

    ident[...] = dot(feats, ws_ref[...]) + bias_ref[...]
    cot = cot_ref[...]
    hgrad[...] = dot(cot, wo_ref[...], ((1,), (1,)))
    runs[ZERO_SLOT] = jnp.zeros((TILE, HID), F32)

    for zd in (0,) + near:
        zs = around(zl, zd)
        for e in near:
            ys = around(y, e)
            arrived(shard(c, ys, zs), p1y.at[ys, zs])
            send(shard(c, ys, zs), shard(c, ys, zs), p1c.at[ys, zs], sibling)
    for yd in range(4):
        for zd in range(4):
            arrived(shard(oc, yd, zd), p1c.at[yd, zd])
    load_values.wait()
    load_index.wait()

    for d in near:
        zs = around(zl, d)
        arrived(xshards(c, y, zs, 1), xgz.at[zs])
    for e in near:
        send(xshards(c, y, 0, 4), xshards(c, y, 0, 4), xgy.at[y], dev(y_=around(y, e)))

    def products(which, pick):
        def step(i, carry):
            total, before = carry
            for u in range(UNROLL):
                p = i * UNROLL + u
                word = idx_s[which, p]
                key = word >> 15
                term = pick((word >> 7) & 255, word & 127)
                total = jnp.where(key == before, total, 0.0) + term
                runs[p] = total
                before = key
            return total, before

        lax.fori_loop(0, NBLK // UNROLL, step, (jnp.zeros((TILE, HID), F32), jnp.int32(-1)))

    products(0, lambda b, o: dot(vals[b], gath[o]))

    def part(j, k):
        return runs[idx_s[1, j * 2 + k]]

    for zz, recv_sems, recv in ((ozh, r3a, recv_a), (zh, r3b, recv_b)):
        for d in near:
            xs = around(x, d)
            j = xs * 2 + zz
            for k in range(2):
                part_send[j, k] = part(j, k).astype(BF16)
            send(part_send.at[j], recv.at[x], recv_sems.at[x], dev(x_=xs))
    for d in near:
        xs = around(x, d)
        arrived(recv_a.at[xs], r3a.at[xs])
    for k in range(2):
        total = part(x * 2 + ozh, k)
        for d in near:
            total = total + recv_a[around(x, d), k].astype(F32)
        zsend[k] = total.astype(BF16)
    send(zsend, recv_z, r3z.at[0], partner)
    for d in near:
        xs = around(x, d)
        arrived(recv_b.at[xs], r3b.at[xs])
    agg = []
    for k in range(2):
        total = part(x * 2 + zh, k)
        for d in near:
            total = total + recv_b[around(x, d), k].astype(F32)
        agg.append(total)
    arrived(recv_z, r3z.at[0])
    hidden, pgrad = [], []
    for k in range(2):
        here = pl.ds(k * TILE, TILE)
        pre = ident[here, :] + (agg[k] + recv_z[k].astype(F32))
        sig = jax.nn.sigmoid(pre)
        hidden.append((pre * sig).astype(BF16))
        grad = hgrad[here, :] * sig * (1.0 + pre * (1.0 - sig))
        pgrad.append(grad.astype(BF16))
        pgt[rep, k] = grad.T.astype(BF16)

    send(pgt.at[rep], pgt.at[rep], r5z.at[0], partner)
    for d in near:
        send(pgt.at[rep], pgt.at[rep], r5x.at[x], dev(x_=around(x, d)))
    hid = jnp.concatenate(hidden, axis=0)
    pg = jnp.concatenate(pgrad, axis=0)
    for e in near:
        ys = around(y, e)
        arrived(xshards(c, ys, 0, 4), xgy.at[ys])
    send(xshards(c, 0, 0, 16), xshards(c, 0, 0, 16), xgc.at[0], sibling)
    updated_ref[...] = (feats.astype(F32) + dot(hid, wo_ref[...])).astype(BF16)
    base[...] = cot.astype(F32) + dot(pg, ws_ref[...], ((1,), (1,)))
    term_self = dot(feats, pg, ((0,), (0,)))
    term_out = dot(hid, cot, ((0,), (0,)))
    term_bias = jnp.sum(pg.astype(F32).reshape(32, 8, HID), axis=0)
    for cc in range(2):
        m_a[cc, :, 0:8, :] = term_self[cc * 128:(cc + 1) * 128, :].reshape(16, 8, HID)
        m_a[cc, :, 8:16, :] = term_out[:, cc * 128:(cc + 1) * 128].reshape(16, 8, HID)
        m_a[cc, :, 16:24, :] = jnp.broadcast_to(term_bias[None], (16, 8, HID))

    spot = zl * 4 + y
    far = [(a, b) for a in range(4) for b in range(4) if (a, b) != (0, 0)]

    def grads_core(m, m_recv, sem):
        send(m.at[oc], m_recv, sem.at[0], sibling)

    def grads_rows(m, m_recv, m_in, sem_c, sem):
        arrived(m_recv, sem_c.at[0])
        m_recv[...] = m_recv[...] + m[c]
        m_in[spot] = m_recv[spot]
        for a, b in far:
            zt, yt = around(zl, a), around(y, b)
            send(m_recv.at[zt * 4 + yt], m_in.at[spot], sem.at[spot], dev(zl_=zt, y_=yt))

    def grads_rep(m_in, m_rep, sem_in, sem):
        for a, b in far:
            q = around(zl, a) * 4 + around(y, b)
            arrived(m_in.at[q], sem_in.at[q])
        total = m_in[0]
        for q in range(1, 16):
            total = total + m_in[q]
        m_rep[rep] = total
        for d in range(1, 8):
            j = (rep + d) % 8
            send(m_rep.at[rep], m_rep.at[rep], sem.at[rep], dev(x_=j // 2, zh_=j % 2))

    def grads_out(m_rep, m_fin, sem_rep, sem):
        for d in range(1, 8):
            j = (rep + d) % 8
            arrived(m_rep.at[j], sem_rep.at[j])
        total = m_rep[0]
        for j in range(1, 8):
            total = total + m_rep[j]
        m_fin[c, spot] = total
        for a, b in far:
            zt, yt = around(zl, a), around(y, b)
            send(m_fin.at[c, spot], m_fin.at[c, spot], sem.at[spot], dev(zl_=zt, y_=yt))

    def grads_last(m_fin, sem_out, sem_f):
        for a, b in far:
            q = around(zl, a) * 4 + around(y, b)
            arrived(m_fin.at[c, q], sem_out.at[q])
        send(m_fin.at[c], m_fin.at[c], sem_f.at[0], sibling)

    grads_core(m_a, m_a_recv, aa_c)
    oj = x * 2 + ozh
    arrived(pgt.at[oj], r5z.at[0])
    for d in near:
        send(pgt.at[oj], pgt.at[oj], r5f.at[x], dev(x_=around(x, d)))
    grads_rows(m_a, m_a_recv, m_a_in, aa_c, aa_in)
    for d in near:
        xs = around(x, d)
        arrived(pgt.at[xs * 2 + zh], r5x.at[xs])
        arrived(pgt.at[xs * 2 + ozh], r5f.at[xs])

    products(2, lambda b, o: dot(pgt[o >> 1, o & 1], vals[b]))

    grads_rep(m_a_in, m_a_rep, aa_in, aa_rep)

    def column(t):
        return runs[idx_s[3, t]]

    def convert(t, _):
        t_send[t] = column(t).astype(BF16)
        return 0

    for ys in range(4):
        lax.fori_loop(oc * 32 + ys * 8, oc * 32 + ys * 8 + 8, convert, 0)
        send(t_send.at[pl.ds(oc * 32 + ys * 8, 8)], recv_c.at[ys], r7c.at[ys], sibling)
    lax.fori_loop(c * 32, c * 32 + 32, convert, 0)
    arrived(xshards(oc, 0, 0, 16), xgc.at[0])

    def message(i, total):
        for u in range(2):
            s = i * 2 + u
            for k in range(2):
                total = total + dot(t_send[s * 2 + k], xgath[s, k * TILE:(k + 1) * TILE, :])
        return total

    term_msg = lax.fori_loop(0, 16, message, jnp.zeros((HID, FEAT), F32))
    m_b[...] = term_msg.T.reshape(2, 16, 8, HID)
    grads_core(m_b, m_b_recv, ab_c)

    for d in near + (0,):
        ys = around(y, d)
        arrived(recv_c.at[ys], r7c.at[ys])
        for t in range(8):
            y_send[ys, t] = (column(c * 32 + ys * 8 + t) + recv_c[ys, t].astype(F32)).astype(BF16)
        if d:
            send(y_send.at[ys], recv_y.at[y], r7y.at[y], dev(y_=ys))
    grads_rows(m_b, m_b_recv, m_b_in, ab_c, ab_in)
    grads_out(m_a_rep, m_a_fin, aa_rep, aa_out)
    for d in near:
        ys = around(y, d)
        arrived(recv_y.at[ys], r7y.at[ys])
    final = []
    for d in near + (0,):
        zs = around(zl, d)
        for k in range(2):
            total = y_send[y, zs * 2 + k].astype(F32)
            for e in near:
                total = total + recv_y[around(y, e), zs * 2 + k].astype(F32)
            if d:
                z7_send[zs, k] = total.astype(BF16)
            else:
                final.append(total)
        if d:
            send(z7_send.at[zs], recv_z7.at[zl], r7z.at[zl], dev(zl_=zs))
    grads_rep(m_b_in, m_b_rep, ab_in, ab_rep)
    grads_last(m_a_fin, aa_out, aa_f)
    for d in near:
        zs = around(zl, d)
        arrived(recv_z7.at[zs], r7z.at[zs])
    for k in range(2):
        total = final[k]
        for d in near:
            total = total + recv_z7[around(zl, d), k].astype(F32)
        here = pl.ds(k * TILE, TILE)
        gnodes_ref[here, :] = (
            base[here, :] + dot(total.T.astype(BF16), wm_ref[...], ((1,), (1,)))
        ).astype(BF16)

    grads_out(m_b_rep, m_b_fin, ab_rep, ab_out)
    grads_last(m_b_fin, ab_out, ab_f)
    arrived(m_a_fin.at[oc], aa_f.at[0])
    factor = 1.0 / math.sqrt(65536)
    for cc in range(2):
        rows_here = slice(cc * 128, (cc + 1) * 128)
        gself_ref[rows_here, :] = m_a_fin[cc, :, 0:8, :].reshape(128, HID) * factor
        gout_ref[:, rows_here] = m_a_fin[cc, :, 8:16, :].reshape(128, HID) * factor
    gbias_ref[...] = jnp.sum(m_a_fin[0, 0, 16:24, :], axis=0, keepdims=True) * factor
    arrived(m_b_fin.at[oc], ab_f.at[0])
    gmsg_ref[...] = m_b_fin[...].reshape(FEAT, HID) * factor
    for copy in sent:
        copy.wait_send()


def body(x, values, brow, bcol, used, ws, wm, bias, wo, cot):
    vmem = pl.BlockSpec(memory_space=pltpu.VMEM)
    dma = pltpu.SemaphoreType.DMA

    def pieces(n):
        return [
            pltpu.VMEM((2, 16, n, HID), F32),
            pltpu.VMEM((16, n, HID), F32),
            pltpu.VMEM((16, n, HID), F32),
            pltpu.VMEM((8, n, HID), F32),
            pltpu.VMEM((2, 16, n, HID), F32),
        ]

    grad_sems = [dma((1,)), dma((16,)), dma((8,)), dma((16,)), dma((1,))]
    updated, gnodes, gself, gmsg, gout, gbias = pl.pallas_call(
        kernel,
        out_shape=(
            jax.ShapeDtypeStruct((256, FEAT), BF16),
            jax.ShapeDtypeStruct((256, FEAT), BF16),
            jax.ShapeDtypeStruct((FEAT, HID), F32),
            jax.ShapeDtypeStruct((FEAT, HID), F32),
            jax.ShapeDtypeStruct((HID, FEAT), F32),
            jax.ShapeDtypeStruct((1, HID), F32),
        ),
        in_specs=[pl.BlockSpec(memory_space=pltpu.SMEM), vmem, pl.BlockSpec(memory_space=pl.ANY)] + [vmem] * 7,
        out_specs=(vmem,) * 6,
        scratch_shapes=[
            pltpu.VMEM((NBLK, TILE, TILE), BF16),
            pltpu.VMEM((CTILES, TILE, HID), BF16),
            pltpu.VMEM((32, 256, FEAT), BF16),
            pltpu.VMEM((NBLK + 1, TILE, HID), F32),
            pltpu.VMEM((8, NB_PAD), jnp.int32),
            pltpu.SMEM((8, NB_PAD), jnp.int32),
            pltpu.VMEM((256, HID), F32),
            pltpu.VMEM((256, FEAT), F32),
            pltpu.VMEM((256, HID), F32),
            pltpu.VMEM((8, 2, TILE, HID), BF16),
            pltpu.VMEM((4, 2, TILE, HID), BF16),
            pltpu.VMEM((4, 2, TILE, HID), BF16),
            pltpu.VMEM((2, TILE, HID), BF16),
            pltpu.VMEM((2, TILE, HID), BF16),
            pltpu.VMEM((8, 2, HID, TILE), BF16),
            pltpu.VMEM((CTILES, HID, TILE), BF16),
            pltpu.VMEM((4, 8, HID, TILE), BF16),
            pltpu.VMEM((4, 8, HID, TILE), BF16),
            pltpu.VMEM((4, 8, HID, TILE), BF16),
            pltpu.VMEM((4, 2, HID, TILE), BF16),
            pltpu.VMEM((4, 2, HID, TILE), BF16),
            *pieces(SELF_ROWS),
            *pieces(MSG_ROWS),
            dma, dma, dma((160,)),
            dma((4,)), dma((4, 4)), dma((4, 4)), dma((4,)), dma((4,)), dma((1,)),
            dma((4,)), dma((4,)), dma((1,)), dma((4,)), dma((1,)), dma((4,)),
            dma((4,)), dma((4,)), dma((4,)),
            *grad_sems,
            *grad_sems,
        ],
        compiler_params=pltpu.CompilerParams(
            collective_id=0, has_side_effects=True, vmem_limit_bytes=52 * 2**20
        ),
        name="layer",
    )(used, x, values, brow, bcol, ws, wm, bias.reshape(1, HID), wo, cot)
    return updated, gnodes, gself, gmsg, gout, gbias.reshape(HID)


def solution(mesh):
    sharded = P(("rows", "rep"), None)
    in_specs = (
        sharded, P(("rows", "rep"), None, None, None), sharded, sharded, P(("rows", "rep")),
        P(), P(), P(), P(), sharded,
    )
    out_specs = (sharded, sharded, P(), P(), P(), P())
    return jax.shard_map(body, mesh=mesh, in_specs=in_specs, out_specs=out_specs, check_vma=False)
```

```python
import functools
import math

import jax
import jax.numpy as jnp
from jax import lax
from jax.experimental import pallas as pl
from jax.experimental.pallas import tpu as pltpu
from jax.sharding import PartitionSpec as P

FEAT = 256
HID = 128
TILE = 128
NBLK = 176
NB_PAD = 256
BROWS = 16
CTILES = 64
ZERO_SLOT = NBLK
MESH = pl.DeviceIdType.MESH
F32 = jnp.float32
BF16 = jnp.bfloat16
UNROLL = 8
CUT = 192
SELF_ROWS = 24
MSG_ROWS = 8


def dot(a, b, dims=((1,), (0,))):
    return lax.dot_general(a, b, (dims, ((), ())), preferred_element_type=F32)


def kernel(
    used_ref, x_hbm, values_ref, brow_hbm, bcol_hbm, ws_hbm, wm_hbm, bias_hbm, wo_hbm, cot_hbm,
    updated_hbm, gnodes_hbm, gself_hbm, gmsg_hbm, gout_hbm, gbias_hbm,
    updated_ref, gnodes_ref, gself_ref, gmsg_ref, gout_ref, gbias_ref,
    x_ref, brow_ref, bcol_ref, ws_ref, wm_ref, bias_ref, wo_ref, cot_ref,
    vals, gath, xgath, runs, idx_v, idx_s, ident, base, hgrad,
    part_send, recv_a, recv_b, zsend, recv_z, pgt,
    t_send, recv_c, t_sum, recv_ya, za_send, recv_za, recv_zb, yb_send, recv_yb,
    m_a, m_a_in, m_a_rep, m_a_fin, m_b, m_b_in, m_b_rep, m_b_fin,
    in_sems, out_sems, v_sem, i_sem, send_sems,
    p1za, p1ya, p1yb, p1zb, p1ca, p1cb, xgz, xgy,
    r3a, r3b, r3z, r5x, r5z, r5f, r7c, r7ya, r7za, r7zb, r7yb,
    aa_in, aa_rep, aa_out, ab_in, ab_rep, ab_out,
):
    row = lax.axis_index("rows")
    rep = lax.axis_index("rep")
    zl, y, c = row // 8, (row // 2) % 4, row % 2
    x, zh = rep // 2, rep % 2
    oc, ozh = 1 - c, 1 - zh

    def dev(zl_=None, y_=None, c_=None, x_=None, zh_=None):
        zl_ = zl if zl_ is None else zl_
        y_ = y if y_ is None else y_
        c_ = c if c_ is None else c_
        x_ = x if x_ is None else x_
        zh_ = zh if zh_ is None else zh_
        return {"rows": zl_ * 8 + y_ * 2 + c_, "rep": x_ * 2 + zh_}

    def around(i, d):
        return (i + d) % 4

    near = (1, 3, 2)
    sibling = dev(c_=oc)
    partner = dev(zh_=ozh)
    pairs = (
        (x_hbm, x_ref), (wm_hbm, wm_ref), (brow_hbm, brow_ref), (bcol_hbm, bcol_ref),
        (ws_hbm, ws_ref), (bias_hbm, bias_ref), (wo_hbm, wo_ref), (cot_hbm, cot_ref),
    )
    loads = [pltpu.make_async_copy(a, b, in_sems.at[i]) for i, (a, b) in enumerate(pairs)]
    for copy in loads:
        copy.start()
    partners = [partner, sibling]
    for d in near:
        partners += [dev(zl_=around(zl, d)), dev(y_=around(y, d)), dev(x_=around(x, d))]
    barrier = pltpu.get_barrier_semaphore()
    for p in partners:
        pl.semaphore_signal(barrier, inc=1, device_id=p, device_id_type=MESH)
    load_values = pltpu.make_async_copy(values_ref.at[0], vals, v_sem)
    load_values.start()

    sent = []

    def send(src, dst, recv, to):
        copy = pltpu.make_async_remote_copy(
            src_ref=src, dst_ref=dst, send_sem=send_sems.at[len(sent)], recv_sem=recv,
            device_id=to, device_id_type=MESH,
        )
        copy.start()
        sent.append(copy)

    def share(ref, recv, to):
        send(ref, ref, recv, to)

    def arrived(dst, recv):
        pltpu.make_async_remote_copy(
            src_ref=dst, dst_ref=dst, send_sem=send_sems.at[0], recv_sem=recv,
            device_id=sibling, device_id_type=MESH,
        ).wait_recv()

    def head(c_, zl_, y_):
        return gath.at[c_ * 4 + zl_, y_, pl.ds(0, 3)]

    def tail(c_, zl_, y_):
        return gath.at[c_ * 4 + zl_, y_, 3]

    def tails(c_, zl_):
        return gath.at[c_ * 4 + zl_, :, 3]

    loads[0].wait()
    loads[1].wait()
    feats = x_ref[...]
    gath[c * 4 + zl, y] = dot(feats, wm_ref[...]).astype(BF16).reshape(4, 64, HID)
    xgath[zl, y] = feats
    pl.semaphore_wait(barrier, len(partners))
    for d in near:
        share(head(c, zl, y), p1za.at[zl], dev(zl_=around(zl, d)))
    for d in near:
        share(tail(c, zl, y), p1yb.at[y], dev(y_=around(y, d)))
    for d in near:
        share(head(c, zl, y), p1ya.at[zl, y], dev(y_=around(y, d)))
    share(head(c, zl, y), p1ca.at[zl, y], sibling)

    for copy in loads[2:]:
        copy.wait()
    used = used_ref[0]
    idx_v[...] = jnp.zeros_like(idx_v)
    idx_v[0:1, 0:NBLK] = brow_ref[...]
    idx_v[1:2, 0:NBLK] = bcol_ref[...]
    lane = lax.broadcasted_iota(jnp.int32, (1, NB_PAD), 1)
    lanes = lax.broadcasted_iota(jnp.int32, (NB_PAD, NB_PAD), 1)
    usable = lane < used
    rows_of = idx_v[0:1, :]
    cols_of = idx_v[1:2, :]
    source = cols_of >> 1
    tile_of = (((source & 1) * 16 + (source >> 3) * 4 + ((source >> 1) & 3)) << 1) + (cols_of & 1)

    def listing(key, other):
        packed = (((key << 8) + lane) << 7) + other
        along = jnp.broadcast_to(packed, (NB_PAD, NB_PAD))
        down = along.T
        rank = jnp.sum((along < down).astype(jnp.int32), axis=1, keepdims=True)
        ordered = jnp.sum(jnp.where(rank == lanes, down, 0), axis=0, keepdims=True)
        keys = down >> 15
        upto = jnp.sum((keys <= lanes).astype(jnp.int32), axis=0, keepdims=True)
        below = jnp.sum((keys < lanes).astype(jnp.int32), axis=0, keepdims=True)
        return ordered, jnp.where(upto > below, upto - 1, ZERO_SLOT)

    def list_blocks():
        order_f, end_f = listing(jnp.where(usable, rows_of, BROWS), tile_of)
        order_b, end_b = listing(jnp.where(usable, tile_of, CTILES), rows_of)
        idx_v[0:1, :] = order_f
        idx_v[1:2, :] = end_f
        idx_v[2:3, :] = order_b
        idx_v[3:4, :] = end_b

    list_blocks()
    load_index = pltpu.make_async_copy(idx_v, idx_s, i_sem)
    load_index.start()

    def pass_head(d):
        zs = around(zl, d)
        arrived(head(c, zs, y), p1za.at[zs])
        for e in near:
            share(head(c, zs, y), p1ya.at[zs, y], dev(y_=around(y, e)))
        share(head(c, zs, y), p1ca.at[zs, y], sibling)

    pass_head(1)
    for e in near:
        ys = around(y, e)
        arrived(tail(c, zl, ys), p1yb.at[ys])
    for d in near:
        share(tails(c, zl), p1zb.at[zl], dev(zl_=around(zl, d)))
    share(tails(c, zl), p1cb.at[zl], sibling)
    pass_head(3)
    pass_head(2)

    ident[...] = dot(feats, ws_ref[...]) + bias_ref[...]
    cot = cot_ref[...]
    hgrad[...] = dot(cot, wo_ref[...], ((1,), (1,)))
    runs[ZERO_SLOT] = jnp.zeros((TILE, HID), F32)

    for d in (0,) + near:
        zs = around(zl, d)
        for e in near:
            ys = around(y, e)
            arrived(head(c, zs, ys), p1ya.at[zs, ys])
            share(head(c, zs, ys), p1ca.at[zs, ys], sibling)
        if d:
            arrived(tails(c, zs), p1zb.at[zs])
            share(tails(c, zs), p1cb.at[zs], sibling)
    for d in near:
        share(xgath.at[zl, y], xgz.at[zl], dev(zl_=around(zl, d)))
    load_values.wait()
    load_index.wait()
    for zs in range(4):
        arrived(tails(oc, zs), p1cb.at[zs])
        for ys in range(4):
            arrived(head(oc, zs, ys), p1ca.at[zs, ys])

    def products(which, pick):
        def step(i, carry):
            total, before = carry
            for u in range(UNROLL):
                p = i * UNROLL + u
                word = idx_s[which, p]
                key = word >> 15
                term = pick((word >> 7) & 255, word & 127)
                total = jnp.where(key == before, total, 0.0) + term
                runs[p] = total
                before = key
            return total, before

        lax.fori_loop(0, NBLK // UNROLL, step, (jnp.zeros((TILE, HID), F32), jnp.int32(-1)))

    def source_tile(o):
        a, b, q = o >> 3, (o >> 1) & 3, (o & 1) * 2
        return jnp.concatenate([gath[a, b, q], gath[a, b, q + 1]], axis=0)

    products(0, lambda b, o: dot(vals[b], source_tile(o)))

    def part(j, k):
        return runs[idx_s[1, j * 2 + k]]

    for zz, recv_sems, recv in ((ozh, r3a, recv_a), (zh, r3b, recv_b)):
        for k in range(2):
            for d in near:
                xs = around(x, d)
                j = xs * 2 + zz
                part_send[j, k] = part(j, k).astype(BF16)
                send(part_send.at[j, k], recv.at[x, k], recv_sems.at[x, k], dev(x_=xs))
    for d in near:
        zs = around(zl, d)
        arrived(xgath.at[zs, y], xgz.at[zs])
    for e in near:
        share(xgath.at[:, y], xgy.at[y], dev(y_=around(y, e)))

    def summed(recv, recv_sems, zz, k):
        total = part(x * 2 + zz, k)
        for d in near:
            xs = around(x, d)
            arrived(recv.at[xs, k], recv_sems.at[xs, k])
            total = total + recv[xs, k].astype(F32)
        return total

    for k in range(2):
        zsend[k] = summed(recv_a, r3a, ozh, k).astype(BF16)
        send(zsend.at[k], recv_z.at[k], r3z.at[k], partner)
    agg = [summed(recv_b, r3b, zh, k) for k in range(2)]
    hidden, pgrad = [], []
    for k in range(2):
        here = pl.ds(k * TILE, TILE)
        arrived(recv_z.at[k], r3z.at[k])
        pre = ident[here, :] + (agg[k] + recv_z[k].astype(F32))
        sig = jax.nn.sigmoid(pre)
        grad = hgrad[here, :] * sig * (1.0 + pre * (1.0 - sig))
        pgt[rep, k] = grad.T.astype(BF16)
        share(pgt.at[rep, k], r5z.at[k], partner)
        for d in near:
            share(pgt.at[rep, k], r5x.at[x, k], dev(x_=around(x, d)))
        hidden.append((pre * sig).astype(BF16))
        pgrad.append(grad.astype(BF16))

    hid = jnp.concatenate(hidden, axis=0)
    pg = jnp.concatenate(pgrad, axis=0)
    updated_ref[...] = (feats.astype(F32) + dot(hid, wo_ref[...])).astype(BF16)
    base[...] = cot.astype(F32) + dot(pg, ws_ref[...], ((1,), (1,)))
    term_self = dot(feats, pg, ((0,), (0,)))
    term_out = dot(hid, cot, ((0,), (0,)))
    term_bias = jnp.sum(pg.astype(F32).reshape(32, 8, HID), axis=0)
    m_a[:, 0:8, :] = term_self.reshape(32, 8, HID)
    m_a[0:16, 8:16, :] = term_out[:, 0:128].reshape(16, 8, HID)
    m_a[16:32, 8:16, :] = term_out[:, 128:256].reshape(16, 8, HID)
    m_a[:, 16:24, :] = jnp.broadcast_to(term_bias[None], (32, 8, HID))

    oj = x * 2 + ozh
    for k in range(2):
        arrived(pgt.at[oj, k], r5z.at[k])
        for d in near:
            share(pgt.at[oj, k], r5f.at[x, k], dev(x_=around(x, d)))
    for k in range(2):
        for d in near:
            xs = around(x, d)
            arrived(pgt.at[xs * 2 + zh, k], r5x.at[xs, k])
            arrived(pgt.at[xs * 2 + ozh, k], r5f.at[xs, k])

    spot = c * 16 + x * 4 + y
    level = zh * 4 + zl

    def plane():
        for cc in range(2):
            for a in range(4):
                for b in range(4):
                    if (cc, a, b) != (0, 0, 0):
                        ct, xt, yt = (c + cc) % 2, around(x, a), around(y, b)
                        yield ct * 16 + xt * 4 + yt, dev(c_=ct, x_=xt, y_=yt)

    def column_devices():
        for d in range(1, 8):
            z = (level + d) % 8
            yield z, dev(zl_=z % 4, zh_=z // 4)

    def grads_scatter(m, m_in, sem):
        m_in[spot] = m[spot]
        for q, to in plane():
            send(m.at[q], m_in.at[spot], sem.at[spot], to)

    def grads_level(m_in, m_rep, sem_in, sem):
        for q, _ in plane():
            arrived(m_in.at[q], sem_in.at[q])
        total = m_in[0]
        for q in range(1, 32):
            total = total + m_in[q]
        m_rep[level] = total
        for _, to in column_devices():
            share(m_rep.at[level], sem.at[level], to)

    def grads_spread(m_rep, m_fin, sem_rep, sem):
        for z, _ in column_devices():
            arrived(m_rep.at[z], sem_rep.at[z])
        total = m_rep[0]
        for z in range(1, 8):
            total = total + m_rep[z]
        m_fin[spot] = total
        for _, to in plane():
            share(m_fin.at[spot], sem.at[spot], to)

    def grads_end(m_fin, sem_out):
        for q, _ in plane():
            arrived(m_fin.at[q], sem_out.at[q])

    grads_scatter(m_a, m_a_in, aa_in)
    products(2, lambda b, o: dot(pgt[o >> 1, o & 1], vals[b]))

    def column(c_, zl_, y_, k):
        return runs[idx_s[3, ((c_ * 4 + zl_) * 4 + y_) * 2 + k]]

    for d in near + (0,):
        zs = around(zl, d)
        for ys in range(4):
            for k in range(2):
                t_send[zs, ys, k * TILE:(k + 1) * TILE, :] = column(oc, zs, ys, k).astype(BF16)
        send(t_send.at[zs], recv_c.at[zs], r7c.at[zs], sibling)
    grads_level(m_a_in, m_a_rep, aa_in, aa_rep)
    for d in near + (0,):
        zs = around(zl, d)
        arrived(recv_c.at[zs], r7c.at[zs])
        for ys in range(4):
            for k in range(2):
                here = slice(k * TILE, (k + 1) * TILE)
                total = column(c, zs, ys, k) + recv_c[zs, ys, here, :].astype(F32)
                t_sum[zs, ys, here, :] = total.astype(BF16)
        if d:
            send(t_sum.at[zs, :, pl.ds(CUT, 256 - CUT)], recv_zb.at[zl], r7zb.at[zl], dev(zl_=zs))
        for e in near:
            ys = around(y, e)
            send(t_sum.at[zs, ys, pl.ds(0, CUT)], recv_ya.at[y, zs], r7ya.at[y, zs], dev(y_=ys))

    for e in near:
        ys = around(y, e)
        arrived(xgath.at[:, ys], xgy.at[ys])

    def message(zs, total):
        for ys in range(4):
            both = jnp.concatenate([t_sum[zs, ys, 0:TILE, :], t_sum[zs, ys, TILE:256, :]], axis=1)
            total = total + dot(both, xgath[zs, ys])
        return total

    term_msg = lax.fori_loop(0, 4, message, jnp.zeros((HID, FEAT), F32))
    m_b[...] = term_msg.T.reshape(32, 8, HID)
    grads_scatter(m_b, m_b_in, ab_in)

    def heads(zs):
        total = t_sum[zs, y, 0:CUT, :].astype(F32)
        for e in near:
            ys = around(y, e)
            arrived(recv_ya.at[ys, zs], r7ya.at[ys, zs])
            total = total + recv_ya[ys, zs].astype(F32)
        return total

    for d in near:
        zs = around(zl, d)
        za_send[zs] = heads(zs).astype(BF16)
        send(za_send.at[zs], recv_za.at[zl], r7za.at[zl], dev(zl_=zs))
    for d in near:
        zs = around(zl, d)
        arrived(recv_zb.at[zs], r7zb.at[zs])
    for e in near + (0,):
        ys = around(y, e)
        final_b = t_sum[zl, ys, CUT:256, :].astype(F32)
        for d in near:
            final_b = final_b + recv_zb[around(zl, d), ys].astype(F32)
        if e:
            yb_send[ys] = final_b.astype(BF16)
            send(yb_send.at[ys], recv_yb.at[y], r7yb.at[y], dev(y_=ys))
    grads_spread(m_a_rep, m_a_fin, aa_rep, aa_out)
    grads_level(m_b_in, m_b_rep, ab_in, ab_rep)
    final_a = heads(zl)
    for d in near:
        zs = around(zl, d)
        arrived(recv_za.at[zs], r7za.at[zs])
        final_a = final_a + recv_za[zs].astype(F32)
    for e in near:
        ys = around(y, e)
        arrived(recv_yb.at[ys], r7yb.at[ys])
        final_b = final_b + recv_yb[ys].astype(F32)
    second = jnp.concatenate([final_a[TILE:CUT], final_b], axis=0)
    for k, total in enumerate((final_a[0:TILE], second)):
        here = pl.ds(k * TILE, TILE)
        gnodes_ref[here, :] = (
            base[here, :] + dot(total.T.astype(BF16), wm_ref[...], ((1,), (1,)))
        ).astype(BF16)
    stores = [
        pltpu.make_async_copy(a, b, out_sems.at[i])
        for i, (a, b) in enumerate((
            (updated_ref, updated_hbm), (gnodes_ref, gnodes_hbm), (gself_ref, gself_hbm),
            (gout_ref, gout_hbm), (gbias_ref, gbias_hbm), (gmsg_ref, gmsg_hbm),
        ))
    ]
    stores[0].start()
    stores[1].start()
    grads_spread(m_b_rep, m_b_fin, ab_rep, ab_out)
    grads_end(m_a_fin, aa_out)
    factor = 1.0 / math.sqrt(65536)
    gself_ref[...] = m_a_fin[:, 0:8, :].reshape(FEAT, HID) * factor
    gout_ref[:, 0:128] = m_a_fin[0:16, 8:16, :].reshape(HID, 128) * factor
    gout_ref[:, 128:256] = m_a_fin[16:32, 8:16, :].reshape(HID, 128) * factor
    gbias_ref[...] = jnp.sum(m_a_fin[0, 16:24, :], axis=0, keepdims=True) * factor
    for copy in stores[2:5]:
        copy.start()
    grads_end(m_b_fin, ab_out)
    gmsg_ref[...] = m_b_fin[...].reshape(FEAT, HID) * factor
    stores[5].start()
    for copy in sent:
        copy.wait_send()
    for copy in stores:
        copy.wait()


def write_out(*refs):
    ins, outs, held, sems = refs[:6], refs[6:12], refs[12:18], refs[18]
    loads = [pltpu.make_async_copy(ins[i], held[i], sems.at[0, i]) for i in range(6)]
    stores = [pltpu.make_async_copy(held[i], outs[i], sems.at[1, i]) for i in range(6)]
    for copy in loads:
        copy.start()
    for load, store in zip(loads, stores):
        load.wait()
        store.start()
    for copy in stores:
        copy.wait()


def body(x, values, brow, bcol, used, ws, wm, bias, wo, cot):
    dma = pltpu.SemaphoreType.DMA

    def pieces(n):
        return [pltpu.VMEM((m, n, HID), F32) for m in (32, 32, 8, 32)]

    out_shape = (
        jax.ShapeDtypeStruct((256, FEAT), BF16),
        jax.ShapeDtypeStruct((256, FEAT), BF16),
        jax.ShapeDtypeStruct((FEAT, HID), F32),
        jax.ShapeDtypeStruct((FEAT, HID), F32),
        jax.ShapeDtypeStruct((HID, FEAT), F32),
        jax.ShapeDtypeStruct((1, HID), F32),
    )
    hbm = pl.BlockSpec(memory_space=pltpu.HBM)
    results = pl.pallas_call(
        kernel,
        out_shape=out_shape,
        in_specs=[pl.BlockSpec(memory_space=pltpu.SMEM)] + [hbm] * 9,
        out_specs=(hbm,) * 6,
        scratch_shapes=[
            *[pltpu.VMEM(shape.shape, shape.dtype) for shape in out_shape],
            pltpu.VMEM((256, FEAT), BF16),
            pltpu.VMEM((1, NBLK), jnp.int32),
            pltpu.VMEM((1, NBLK), jnp.int32),
            pltpu.VMEM((FEAT, HID), BF16),
            pltpu.VMEM((FEAT, HID), BF16),
            pltpu.VMEM((1, HID), F32),
            pltpu.VMEM((HID, FEAT), BF16),
            pltpu.VMEM((256, FEAT), BF16),
            pltpu.VMEM((NBLK, TILE, TILE), BF16),
            pltpu.VMEM((8, 4, 4, 64, HID), BF16),
            pltpu.VMEM((4, 4, 256, FEAT), BF16),
            pltpu.VMEM((NBLK + 1, TILE, HID), F32),
            pltpu.VMEM((8, NB_PAD), jnp.int32),
            pltpu.SMEM((8, NB_PAD), jnp.int32),
            pltpu.VMEM((256, HID), F32),
            pltpu.VMEM((256, FEAT), F32),
            pltpu.VMEM((256, HID), F32),
            pltpu.VMEM((8, 2, TILE, HID), BF16),
            pltpu.VMEM((4, 2, TILE, HID), BF16),
            pltpu.VMEM((4, 2, TILE, HID), BF16),
            pltpu.VMEM((2, TILE, HID), BF16),
            pltpu.VMEM((2, TILE, HID), BF16),
            pltpu.VMEM((8, 2, HID, TILE), BF16),
            pltpu.VMEM((4, 4, 256, TILE), BF16),
            pltpu.VMEM((4, 4, 256, TILE), BF16),
            pltpu.VMEM((4, 4, 256, TILE), BF16),
            pltpu.VMEM((4, 4, CUT, TILE), BF16),
            pltpu.VMEM((4, CUT, TILE), BF16),
            pltpu.VMEM((4, CUT, TILE), BF16),
            pltpu.VMEM((4, 4, 256 - CUT, TILE), BF16),
            pltpu.VMEM((4, 256 - CUT, TILE), BF16),
            pltpu.VMEM((4, 256 - CUT, TILE), BF16),
            *pieces(SELF_ROWS),
            *pieces(MSG_ROWS),
            dma((8,)), dma((6,)), dma, dma, dma((280,)),
            dma((4,)), dma((4, 4)), dma((4,)), dma((4,)), dma((4, 4)), dma((4,)), dma((4,)), dma((4,)),
            dma((4, 2)), dma((4, 2)), dma((2,)), dma((4, 2)), dma((2,)), dma((4, 2)),
            dma((4,)), dma((4, 4)), dma((4,)), dma((4,)), dma((4,)),
            dma((32,)), dma((8,)), dma((32,)),
            dma((32,)), dma((8,)), dma((32,)),
        ],
        compiler_params=pltpu.CompilerParams(
            collective_id=0, has_side_effects=True, vmem_limit_bytes=63 * 2**20
        ),
        name="layer",
    )(used, x, values, brow, bcol, ws, wm, bias.reshape(1, HID), wo, cot)
    updated, gnodes, gself, gmsg, gout, gbias = pl.pallas_call(
        write_out,
        out_shape=out_shape,
        in_specs=[hbm] * 6,
        out_specs=(hbm,) * 6,
        scratch_shapes=[*[pltpu.VMEM(shape.shape, shape.dtype) for shape in out_shape], dma((2, 6))],
        name="write_out",
    )(*results)
    return updated, gnodes, gself, gmsg, gout, gbias.reshape(HID)


def solution(mesh):
    sharded = P(("rows", "rep"), None)
    in_specs = (
        sharded, P(("rows", "rep"), None, None, None), sharded, sharded, P(("rows", "rep")),
        P(), P(), P(), P(), sharded,
    )
    out_specs = (sharded, sharded, P(), P(), P(), P())
    return jax.shard_map(body, mesh=mesh, in_specs=in_specs, out_specs=out_specs, check_vma=False)
```

```python
import functools
import math

import jax
import jax.numpy as jnp
from jax import lax
from jax.experimental import pallas as pl
from jax.experimental.pallas import tpu as pltpu
from jax.sharding import PartitionSpec as P

FEAT = 256
HID = 128
TILE = 128
NBLK = 176
NB_PAD = 256
BROWS = 16
CTILES = 64
ZERO_SLOT = NBLK
MESH = pl.DeviceIdType.MESH
F32 = jnp.float32
BF16 = jnp.bfloat16
UNROLL = 44
CUT = 192


def dot(a, b, dims=((1,), (0,))):
    return lax.dot_general(a, b, (dims, ((), ())), preferred_element_type=F32)


def kernel(
    used_ref, x_hbm, values_ref, brow_hbm, bcol_hbm, ws_hbm, wm_hbm, bias_hbm, wo_hbm, cot_hbm,
    updated_hbm, gnodes_hbm, gself_hbm, gmsg_hbm, gout_hbm, gbias_hbm,
    updated_ref, gnodes_ref, gself_ref, gmsg_ref, gout_ref, gbias_ref,
    x_ref, brow_ref, bcol_ref, ws_ref, wm_ref, bias_ref, wo_ref, cot_ref,
    vals, gath, xgath, runs, idx_v, idx_s, ident, base, hgrad,
    part_send, recv_a, recv_b, zsend, recv_z, pgt,
    t_send, recv_c, t_sum, recv_ya, za_send, recv_za, recv_zb, yb_send, recv_yb,
    m_a, a_core, a_y, a_x, m_a_rep, m_a_fin, m_b, m_b_in, m_b_rep, m_b_fin,
    in_sems, out_sems, v_sem, i_sem, send_sems,
    p1za, p1ya, p1yb, p1zb, p1ca, p1cb, xgz, xgy,
    r3a, r3b, r3z, r5x, r5z, r5f, r7c, r7ya, r7za, r7zb, r7yb,
    aa_c, aa_y, aa_x, aa_z, aa_ox, aa_oy, aa_oc, ab_in, ab_rep, ab_out,
):
    row = lax.axis_index("rows")
    rep = lax.axis_index("rep")
    zl, y, c = row // 8, (row // 2) % 4, row % 2
    x, zh = rep // 2, rep % 2
    oc, ozh = 1 - c, 1 - zh

    def dev(zl_=None, y_=None, c_=None, x_=None, zh_=None):
        zl_ = zl if zl_ is None else zl_
        y_ = y if y_ is None else y_
        c_ = c if c_ is None else c_
        x_ = x if x_ is None else x_
        zh_ = zh if zh_ is None else zh_
        return {"rows": zl_ * 8 + y_ * 2 + c_, "rep": x_ * 2 + zh_}

    def around(i, d):
        return (i + d) % 4

    near = (1, 3, 2)
    sibling = dev(c_=oc)
    partner = dev(zh_=ozh)
    pairs = (
        (x_hbm, x_ref), (wm_hbm, wm_ref), (brow_hbm, brow_ref), (bcol_hbm, bcol_ref),
        (ws_hbm, ws_ref), (bias_hbm, bias_ref), (wo_hbm, wo_ref), (cot_hbm, cot_ref),
    )
    loads = [pltpu.make_async_copy(a, b, in_sems.at[i]) for i, (a, b) in enumerate(pairs)]
    for copy in loads:
        copy.start()
    partners = [partner, sibling]
    for d in near:
        partners += [dev(zl_=around(zl, d)), dev(y_=around(y, d)), dev(x_=around(x, d))]
    barrier = pltpu.get_barrier_semaphore()
    for p in partners:
        pl.semaphore_signal(barrier, inc=1, device_id=p, device_id_type=MESH)
    load_values = pltpu.make_async_copy(values_ref.at[0], vals, v_sem)
    load_values.start()

    sent = []

    def send(src, dst, recv, to):
        copy = pltpu.make_async_remote_copy(
            src_ref=src, dst_ref=dst, send_sem=send_sems.at[len(sent)], recv_sem=recv,
            device_id=to, device_id_type=MESH,
        )
        copy.start()
        sent.append(copy)

    def share(ref, recv, to):
        send(ref, ref, recv, to)

    def arrived(dst, recv):
        pltpu.make_async_remote_copy(
            src_ref=dst, dst_ref=dst, send_sem=send_sems.at[0], recv_sem=recv,
            device_id=sibling, device_id_type=MESH,
        ).wait_recv()

    def head(c_, zl_, y_):
        return gath.at[c_ * 4 + zl_, y_, pl.ds(0, 3)]

    def tail(c_, zl_, y_):
        return gath.at[c_ * 4 + zl_, y_, 3]

    def tails(c_, zl_):
        return gath.at[c_ * 4 + zl_, :, 3]

    loads[0].wait()
    loads[1].wait()
    feats = x_ref[...]
    gath[c * 4 + zl, y] = dot(feats, wm_ref[...]).astype(BF16).reshape(4, 64, HID)
    xgath[zl, y] = feats
    pl.semaphore_wait(barrier, len(partners))
    for d in near:
        share(head(c, zl, y), p1za.at[zl], dev(zl_=around(zl, d)))
    for d in near:
        share(tail(c, zl, y), p1yb.at[y], dev(y_=around(y, d)))
    for d in near:
        share(head(c, zl, y), p1ya.at[zl, y], dev(y_=around(y, d)))
    share(head(c, zl, y), p1ca.at[zl, y], sibling)

    for copy in loads[2:]:
        copy.wait()
    used = used_ref[0]
    idx_v[...] = jnp.zeros_like(idx_v)
    idx_v[0:1, 0:NBLK] = brow_ref[...]
    idx_v[1:2, 0:NBLK] = bcol_ref[...]
    lane = lax.broadcasted_iota(jnp.int32, (1, NB_PAD), 1)
    lanes = lax.broadcasted_iota(jnp.int32, (NB_PAD, NB_PAD), 1)
    usable = lane < used
    rows_of = idx_v[0:1, :]
    cols_of = idx_v[1:2, :]
    source = cols_of >> 1
    tile_of = (((source & 1) * 16 + (source >> 3) * 4 + ((source >> 1) & 3)) << 1) + (cols_of & 1)

    def listing(key, other):
        packed = (((key << 8) + lane) << 7) + other
        along = jnp.broadcast_to(packed, (NB_PAD, NB_PAD))
        down = along.T
        rank = jnp.sum((along < down).astype(jnp.int32), axis=1, keepdims=True)
        ordered = jnp.sum(jnp.where(rank == lanes, down, 0), axis=0, keepdims=True)
        keys = down >> 15
        upto = jnp.sum((keys <= lanes).astype(jnp.int32), axis=0, keepdims=True)
        below = jnp.sum((keys < lanes).astype(jnp.int32), axis=0, keepdims=True)
        return ordered, jnp.where(upto > below, upto - 1, ZERO_SLOT)

    def list_blocks():
        order_f, end_f = listing(jnp.where(usable, rows_of, BROWS), tile_of)
        order_b, end_b = listing(jnp.where(usable, tile_of, CTILES), rows_of)
        idx_v[0:1, :] = order_f
        idx_v[1:2, :] = end_f
        idx_v[2:3, :] = order_b
        idx_v[3:4, :] = end_b

    list_blocks()
    load_index = pltpu.make_async_copy(idx_v, idx_s, i_sem)
    load_index.start()

    def pass_head(d):
        zs = around(zl, d)
        arrived(head(c, zs, y), p1za.at[zs])
        for e in near:
            share(head(c, zs, y), p1ya.at[zs, y], dev(y_=around(y, e)))
        share(head(c, zs, y), p1ca.at[zs, y], sibling)

    pass_head(1)
    for e in near:
        ys = around(y, e)
        arrived(tail(c, zl, ys), p1yb.at[ys])
    for d in near:
        share(tails(c, zl), p1zb.at[zl], dev(zl_=around(zl, d)))
    share(tails(c, zl), p1cb.at[zl], sibling)
    pass_head(3)
    pass_head(2)
    for d in near:
        share(xgath.at[zl, y], xgz.at[zl], dev(zl_=around(zl, d)))

    ident[...] = dot(feats, ws_ref[...]) + bias_ref[...]
    cot = cot_ref[...]
    hgrad[...] = dot(cot, wo_ref[...], ((1,), (1,)))
    runs[ZERO_SLOT] = jnp.zeros((TILE, HID), F32)

    for d in (0,) + near:
        zs = around(zl, d)
        for e in near:
            ys = around(y, e)
            arrived(head(c, zs, ys), p1ya.at[zs, ys])
            share(head(c, zs, ys), p1ca.at[zs, ys], sibling)
        if d:
            arrived(tails(c, zs), p1zb.at[zs])
            share(tails(c, zs), p1cb.at[zs], sibling)
    load_values.wait()
    load_index.wait()
    for zs in range(4):
        arrived(tails(oc, zs), p1cb.at[zs])
        for ys in range(4):
            arrived(head(oc, zs, ys), p1ca.at[zs, ys])

    def pass_raw(steps):
        for d in steps:
            zs = around(zl, d)
            if d:
                arrived(xgath.at[zs, y], xgz.at[zs])
            for e in near:
                share(xgath.at[zs, y], xgy.at[zs, y], dev(y_=around(y, e)))

    pass_raw((0,))

    def products(which, pick):
        def step(i, carry):
            total, before = carry
            for u in range(UNROLL):
                p = i * UNROLL + u
                word = idx_s[which, p]
                key = word >> 15
                term = pick((word >> 7) & 255, word & 127)
                total = jnp.where(key == before, total, 0.0) + term
                runs[p] = total
                before = key
            return total, before

        lax.fori_loop(0, NBLK // UNROLL, step, (jnp.zeros((TILE, HID), F32), jnp.int32(-1)))

    def source_tile(o):
        a, b, q = o >> 3, (o >> 1) & 3, (o & 1) * 2
        return jnp.concatenate([gath[a, b, q], gath[a, b, q + 1]], axis=0)

    products(0, lambda b, o: dot(vals[b], source_tile(o)))

    def part(j, k):
        return runs[idx_s[1, j * 2 + k]]

    for zz, recv_sems, recv in ((ozh, r3a, recv_a), (zh, r3b, recv_b)):
        for k in range(2):
            for d in near:
                xs = around(x, d)
                j = xs * 2 + zz
                part_send[j, k] = part(j, k).astype(BF16)
                send(part_send.at[j, k], recv.at[x, k], recv_sems.at[x, k], dev(x_=xs))

    pass_raw((1, 3))

    def summed(recv, recv_sems, zz, k):
        total = part(x * 2 + zz, k)
        for d in near:
            xs = around(x, d)
            arrived(recv.at[xs, k], recv_sems.at[xs, k])
            total = total + recv[xs, k].astype(F32)
        return total

    for k in range(2):
        zsend[k] = summed(recv_a, r3a, ozh, k).astype(BF16)
        send(zsend.at[k], recv_z.at[k], r3z.at[k], partner)
    pass_raw((2,))
    agg = [summed(recv_b, r3b, zh, k) for k in range(2)]
    hidden, pgrad = [], []
    for k in range(2):
        here = pl.ds(k * TILE, TILE)
        arrived(recv_z.at[k], r3z.at[k])
        pre = ident[here, :] + (agg[k] + recv_z[k].astype(F32))
        sig = jax.nn.sigmoid(pre)
        grad = hgrad[here, :] * sig * (1.0 + pre * (1.0 - sig))
        pgt[rep, k] = grad.T.astype(BF16)
        share(pgt.at[rep, k], r5z.at[k], partner)
        for d in near:
            share(pgt.at[rep, k], r5x.at[x, k], dev(x_=around(x, d)))
        hidden.append((pre * sig).astype(BF16))
        pgrad.append(grad.astype(BF16))

    hid = jnp.concatenate(hidden, axis=0)
    pg = jnp.concatenate(pgrad, axis=0)
    updated_ref[...] = (feats.astype(F32) + dot(hid, wo_ref[...])).astype(BF16)
    base[...] = cot.astype(F32) + dot(pg, ws_ref[...], ((1,), (1,)))
    term_self = dot(feats, pg, ((0,), (0,)))
    term_out = dot(hid, cot, ((0,), (0,)))
    term_bias = jnp.sum(pg.astype(F32).reshape(32, 8, HID), axis=0)
    for h in range(2):
        m_a[h, :, :, 0:8, :] = term_self[h * 128:(h + 1) * 128, :].reshape(4, 4, 8, HID)
        m_a[h, :, :, 8:16, :] = term_out[:, h * 128:(h + 1) * 128].reshape(4, 4, 8, HID)
        m_a[h, :, :, 16:24, :] = jnp.broadcast_to(term_bias[None, None], (4, 4, 8, HID))
    send(m_a.at[oc], a_core, aa_c.at[0], sibling)

    oj = x * 2 + ozh
    for k in range(2):
        arrived(pgt.at[oj, k], r5z.at[k])
        for d in near:
            share(pgt.at[oj, k], r5f.at[x, k], dev(x_=around(x, d)))
    spot = c * 16 + x * 4 + y
    level = zh * 4 + zl

    def plane():
        for a in (2, 1, 3, 0):
            for b in (2, 1, 3, 0):
                for cc in (1, 0):
                    if (cc, a, b) != (0, 0, 0):
                        ct, xt, yt = (c + cc) % 2, around(x, a), around(y, b)
                        yield ct * 16 + xt * 4 + yt, dev(c_=ct, x_=xt, y_=yt)

    def column_devices():
        for d in (4, 3, 5, 2, 6, 1, 7):
            z = (level + d) % 8
            yield z, dev(zl_=z % 4, zh_=z // 4)

    def grads_scatter(m, m_in, sem):
        m_in[spot] = m[spot]
        for q, to in plane():
            send(m.at[q], m_in.at[spot], sem.at[spot], to)

    def grads_level(m_in, m_rep, sem_in, sem):
        for q, _ in plane():
            arrived(m_in.at[q], sem_in.at[q])
        total = m_in[0]
        for q in range(1, 32):
            total = total + m_in[q]
        m_rep[level] = total
        for _, to in column_devices():
            share(m_rep.at[level], sem.at[level], to)

    def grads_spread(m_rep, m_fin, sem_rep, sem):
        for z, _ in column_devices():
            arrived(m_rep.at[z], sem_rep.at[z])
        total = m_rep[0]
        for z in range(1, 8):
            total = total + m_rep[z]
        m_fin[spot] = total
        for _, to in plane():
            share(m_fin.at[spot], sem.at[spot], to)

    def grads_end(m_fin, sem_out):
        for q, _ in plane():
            arrived(m_fin.at[q], sem_out.at[q])

    def sums_x():
        arrived(a_core, aa_c.at[0])
        a_core[...] = a_core[...] + m_a[c]
        for d in near:
            xs = around(x, d)
            send(a_core.at[xs], a_x.at[x], aa_x.at[x], dev(x_=xs))

    def sums_y():
        total = a_core[x]
        for d in near:
            xs = around(x, d)
            arrived(a_x.at[xs], aa_x.at[xs])
            total = total + a_x[xs]
        a_x[x] = total
        for d in near:
            ys = around(y, d)
            send(a_x.at[x, ys], a_y.at[y], aa_y.at[y], dev(y_=ys))

    def sums_z():
        total = a_x[x, y]
        for d in near:
            ys = around(y, d)
            arrived(a_y.at[ys], aa_y.at[ys])
            total = total + a_y[ys]
        m_a_rep[level] = total
        for _, to in column_devices():
            share(m_a_rep.at[level], aa_z.at[level], to)

    def spread_x():
        for z, _ in column_devices():
            arrived(m_a_rep.at[z], aa_z.at[z])
        total = m_a_rep[0]
        for z in range(1, 8):
            total = total + m_a_rep[z]
        m_a_fin[c, x, y] = total
        for d in near:
            share(m_a_fin.at[c, x, y], aa_ox.at[x], dev(x_=around(x, d)))

    def spread_y():
        for d in near:
            xs = around(x, d)
            arrived(m_a_fin.at[c, xs, y], aa_ox.at[xs])
        for d in near:
            share(m_a_fin.at[c, :, y], aa_oy.at[y], dev(y_=around(y, d)))

    def spread_core():
        for d in near:
            ys = around(y, d)
            arrived(m_a_fin.at[c, :, ys], aa_oy.at[ys])
        share(m_a_fin.at[c], aa_oc.at[0], sibling)

    sums_x()
    for k in range(2):
        for d in near:
            xs = around(x, d)
            arrived(pgt.at[xs * 2 + zh, k], r5x.at[xs, k])
            arrived(pgt.at[xs * 2 + ozh, k], r5f.at[xs, k])
    sums_y()
    products(2, lambda b, o: dot(pgt[o >> 1, o & 1], vals[b]))
    sums_z()

    def column(c_, zl_, y_, k):
        return runs[idx_s[3, ((c_ * 4 + zl_) * 4 + y_) * 2 + k]]

    for d in near + (0,):
        zs = around(zl, d)
        for ys in range(4):
            for k in range(2):
                t_send[zs, ys, k * TILE:(k + 1) * TILE, :] = column(oc, zs, ys, k).astype(BF16)
        send(t_send.at[zs], recv_c.at[zs], r7c.at[zs], sibling)
    def send_heads(zs):
        for e in near:
            ys = around(y, e)
            send(t_sum.at[zs, ys, pl.ds(0, CUT)], recv_ya.at[y, zs], r7ya.at[y, zs], dev(y_=ys))

    for d in near + (0,):
        zs = around(zl, d)
        arrived(recv_c.at[zs], r7c.at[zs])
        for ys in range(4):
            for k in range(2):
                here = slice(k * TILE, (k + 1) * TILE)
                total = column(c, zs, ys, k) + recv_c[zs, ys, here, :].astype(F32)
                t_sum[zs, ys, here, :] = total.astype(BF16)
        if d:
            send(t_sum.at[zs, :, pl.ds(CUT, 256 - CUT)], recv_zb.at[zl], r7zb.at[zl], dev(zl_=zs))
        if d in (1, 3):
            send_heads(zs)

    for e in near:
        ys = around(y, e)
        for zs in range(4):
            arrived(xgath.at[zs, ys], xgy.at[zs, ys])

    def message(zs, total):
        for ys in range(4):
            both = jnp.concatenate([t_sum[zs, ys, 0:TILE, :], t_sum[zs, ys, TILE:256, :]], axis=1)
            total = total + dot(both, xgath[zs, ys])
        return total

    term_msg = lax.fori_loop(0, 4, message, jnp.zeros((HID, FEAT), F32))
    m_b[...] = term_msg.T.reshape(32, 8, HID)
    grads_scatter(m_b, m_b_in, ab_in)
    for d in (2, 0):
        send_heads(around(zl, d))
    spread_x()

    def heads(zs):
        total = t_sum[zs, y, 0:CUT, :].astype(F32)
        for e in near:
            ys = around(y, e)
            arrived(recv_ya.at[ys, zs], r7ya.at[ys, zs])
            total = total + recv_ya[ys, zs].astype(F32)
        return total

    for d in near:
        zs = around(zl, d)
        za_send[zs] = heads(zs).astype(BF16)
        send(za_send.at[zs], recv_za.at[zl], r7za.at[zl], dev(zl_=zs))
    spread_y()
    grads_level(m_b_in, m_b_rep, ab_in, ab_rep)
    for d in near:
        zs = around(zl, d)
        arrived(recv_zb.at[zs], r7zb.at[zs])
    for e in near + (0,):
        ys = around(y, e)
        final_b = t_sum[zl, ys, CUT:256, :].astype(F32)
        for d in near:
            final_b = final_b + recv_zb[around(zl, d), ys].astype(F32)
        if e:
            yb_send[ys] = final_b.astype(BF16)
            send(yb_send.at[ys], recv_yb.at[y], r7yb.at[y], dev(y_=ys))
    spread_core()
    final_a = heads(zl)
    for d in near:
        zs = around(zl, d)
        arrived(recv_za.at[zs], r7za.at[zs])
        final_a = final_a + recv_za[zs].astype(F32)
    for e in near:
        ys = around(y, e)
        arrived(recv_yb.at[ys], r7yb.at[ys])
        final_b = final_b + recv_yb[ys].astype(F32)
    grads_spread(m_b_rep, m_b_fin, ab_rep, ab_out)
    second = jnp.concatenate([final_a[TILE:CUT], final_b], axis=0)
    for k, total in enumerate((final_a[0:TILE], second)):
        here = pl.ds(k * TILE, TILE)
        gnodes_ref[here, :] = (
            base[here, :] + dot(total.T.astype(BF16), wm_ref[...], ((1,), (1,)))
        ).astype(BF16)
    stores = [
        pltpu.make_async_copy(a, b, out_sems.at[i])
        for i, (a, b) in enumerate((
            (updated_ref, updated_hbm), (gnodes_ref, gnodes_hbm), (gself_ref, gself_hbm),
            (gout_ref, gout_hbm), (gbias_ref, gbias_hbm), (gmsg_ref, gmsg_hbm),
        ))
    ]
    stores[0].start()
    stores[1].start()
    arrived(m_a_fin.at[oc], aa_oc.at[0])
    factor = 1.0 / math.sqrt(65536)
    for h in range(2):
        half = slice(h * 128, (h + 1) * 128)
        gself_ref[half, :] = m_a_fin[h, :, :, 0:8, :].reshape(128, HID) * factor
        gout_ref[:, half] = m_a_fin[h, :, :, 8:16, :].reshape(HID, 128) * factor
    gbias_ref[...] = jnp.sum(m_a_fin[0, 0, 0, 16:24, :], axis=0, keepdims=True) * factor
    for copy in stores[2:5]:
        copy.start()
    grads_end(m_b_fin, ab_out)
    gmsg_ref[...] = m_b_fin[...].reshape(FEAT, HID) * factor
    stores[5].start()
    for copy in sent:
        copy.wait_send()
    for copy in stores:
        copy.wait()


def write_out(*refs):
    ins, outs, held, sems = refs[:6], refs[6:12], refs[12:18], refs[18]
    loads = [pltpu.make_async_copy(ins[i], held[i], sems.at[0, i]) for i in range(6)]
    stores = [pltpu.make_async_copy(held[i], outs[i], sems.at[1, i]) for i in range(6)]
    for copy in loads:
        copy.start()
    for load, store in zip(loads, stores):
        load.wait()
        store.start()
    for copy in stores:
        copy.wait()


def body(x, values, brow, bcol, used, ws, wm, bias, wo, cot):
    dma = pltpu.SemaphoreType.DMA

    out_shape = (
        jax.ShapeDtypeStruct((256, FEAT), BF16),
        jax.ShapeDtypeStruct((256, FEAT), BF16),
        jax.ShapeDtypeStruct((FEAT, HID), F32),
        jax.ShapeDtypeStruct((FEAT, HID), F32),
        jax.ShapeDtypeStruct((HID, FEAT), F32),
        jax.ShapeDtypeStruct((1, HID), F32),
    )
    hbm = pl.BlockSpec(memory_space=pltpu.HBM)
    results = pl.pallas_call(
        kernel,
        out_shape=out_shape,
        in_specs=[pl.BlockSpec(memory_space=pltpu.SMEM)] + [hbm] * 9,
        out_specs=(hbm,) * 6,
        scratch_shapes=[
            *[pltpu.VMEM(shape.shape, shape.dtype) for shape in out_shape],
            pltpu.VMEM((256, FEAT), BF16),
            pltpu.VMEM((1, NBLK), jnp.int32),
            pltpu.VMEM((1, NBLK), jnp.int32),
            pltpu.VMEM((FEAT, HID), BF16),
            pltpu.VMEM((FEAT, HID), BF16),
            pltpu.VMEM((1, HID), F32),
            pltpu.VMEM((HID, FEAT), BF16),
            pltpu.VMEM((256, FEAT), BF16),
            pltpu.VMEM((NBLK, TILE, TILE), BF16),
            pltpu.VMEM((8, 4, 4, 64, HID), BF16),
            pltpu.VMEM((4, 4, 256, FEAT), BF16),
            pltpu.VMEM((NBLK + 1, TILE, HID), F32),
            pltpu.VMEM((8, NB_PAD), jnp.int32),
            pltpu.SMEM((8, NB_PAD), jnp.int32),
            pltpu.VMEM((256, HID), F32),
            pltpu.VMEM((256, FEAT), F32),
            pltpu.VMEM((256, HID), F32),
            pltpu.VMEM((8, 2, TILE, HID), BF16),
            pltpu.VMEM((4, 2, TILE, HID), BF16),
            pltpu.VMEM((4, 2, TILE, HID), BF16),
            pltpu.VMEM((2, TILE, HID), BF16),
            pltpu.VMEM((2, TILE, HID), BF16),
            pltpu.VMEM((8, 2, HID, TILE), BF16),
            pltpu.VMEM((4, 4, 256, TILE), BF16),
            pltpu.VMEM((4, 4, 256, TILE), BF16),
            pltpu.VMEM((4, 4, 256, TILE), BF16),
            pltpu.VMEM((4, 4, CUT, TILE), BF16),
            pltpu.VMEM((4, CUT, TILE), BF16),
            pltpu.VMEM((4, CUT, TILE), BF16),
            pltpu.VMEM((4, 4, 256 - CUT, TILE), BF16),
            pltpu.VMEM((4, 256 - CUT, TILE), BF16),
            pltpu.VMEM((4, 256 - CUT, TILE), BF16),
            *[pltpu.VMEM((*lead, 24, HID), F32) for lead in ((2, 4, 4), (4, 4), (4,), (4, 4), (8,), (2, 4, 4))],
            *[pltpu.VMEM((lead, 8, HID), F32) for lead in (32, 32, 8, 32)],
            dma((8,)), dma((6,)), dma, dma, dma((280,)),
            dma((4,)), dma((4, 4)), dma((4,)), dma((4,)), dma((4, 4)), dma((4,)), dma((4,)), dma((4, 4)),
            dma((4, 2)), dma((4, 2)), dma((2,)), dma((4, 2)), dma((2,)), dma((4, 2)),
            dma((4,)), dma((4, 4)), dma((4,)), dma((4,)), dma((4,)),
            dma((1,)), dma((4,)), dma((4,)), dma((8,)), dma((4,)), dma((4,)), dma((1,)),
            dma((32,)), dma((8,)), dma((32,)),
        ],
        compiler_params=pltpu.CompilerParams(
            collective_id=0, has_side_effects=True, vmem_limit_bytes=63 * 2**20
        ),
        name="layer",
    )(used, x, values, brow, bcol, ws, wm, bias.reshape(1, HID), wo, cot)
    updated, gnodes, gself, gmsg, gout, gbias = pl.pallas_call(
        write_out,
        out_shape=out_shape,
        in_specs=[hbm] * 6,
        out_specs=(hbm,) * 6,
        scratch_shapes=[*[pltpu.VMEM(shape.shape, shape.dtype) for shape in out_shape], dma((2, 6))],
        name="write_out",
    )(*results)
    return updated, gnodes, gself, gmsg, gout, gbias.reshape(HID)


def solution(mesh):
    sharded = P(("rows", "rep"), None)
    in_specs = (
        sharded, P(("rows", "rep"), None, None, None), sharded, sharded, P(("rows", "rep")),
        P(), P(), P(), P(), sharded,
    )
    out_specs = (sharded, sharded, P(), P(), P(), P())
    return jax.shard_map(body, mesh=mesh, in_specs=in_specs, out_specs=out_specs, check_vma=False)
```

```python
import functools
import math

import jax
import jax.numpy as jnp
from jax import lax
from jax.experimental import pallas as pl
from jax.experimental.pallas import tpu as pltpu
from jax.sharding import PartitionSpec as P

FEAT = 256
HID = 128
TILE = 128
NBLK = 176
NB_PAD = 256
BROWS = 16
CTILES = 64
ZERO_SLOT = NBLK
MESH = pl.DeviceIdType.MESH
F32 = jnp.float32
BF16 = jnp.bfloat16
UNROLL = 44
CUT = 192


def dot(a, b, dims=((1,), (0,))):
    return lax.dot_general(a, b, (dims, ((), ())), preferred_element_type=F32)


def kernel(
    used_ref, x_hbm, values_ref, brow_hbm, bcol_hbm, ws_hbm, wm_hbm, bias_hbm, wo_hbm, cot_hbm,
    updated_hbm, gnodes_hbm, gself_hbm, gmsg_hbm, gout_hbm, gbias_hbm,
    updated_ref, gnodes_ref, gself_ref, gmsg_ref, gout_ref, gbias_ref,
    x_ref, brow_ref, bcol_ref, ws_ref, wm_ref, bias_ref, wo_ref, cot_ref,
    vals, gath, xgath, runs, idx_v, idx_s, ident, base, hgrad,
    part_send, recv_a, recv_b, zsend, recv_z, pgt,
    t_send, recv_c, t_sum, recv_ya, za_send, recv_za, recv_zb, yb_send, recv_yb,
    m_a, a_core, a_y, a_x, m_a_rep, m_a_fin, m_b, m_b_in, m_b_rep, m_b_fin,
    in_sems, out_sems, v_sem, i_sem, send_sems,
    p1za, p1ya, p1yb, p1zb, p1ca, p1cb, xgz, xgy,
    r3a, r3b, r3z, r5x, r5z, r5f, r7c, r7ya, r7za, r7zb, r7yb,
    aa_c, aa_y, aa_x, aa_z, aa_ox, aa_oy, aa_oc, ab_in, ab_rep, ab_out,
):
    row = lax.axis_index("rows")
    rep = lax.axis_index("rep")
    zl, y, c = row // 8, (row // 2) % 4, row % 2
    x, zh = rep // 2, rep % 2
    oc, ozh = 1 - c, 1 - zh

    def dev(zl_=None, y_=None, c_=None, x_=None, zh_=None):
        zl_ = zl if zl_ is None else zl_
        y_ = y if y_ is None else y_
        c_ = c if c_ is None else c_
        x_ = x if x_ is None else x_
        zh_ = zh if zh_ is None else zh_
        return {"rows": zl_ * 8 + y_ * 2 + c_, "rep": x_ * 2 + zh_}

    def around(i, d):
        return (i + d) % 4

    near = (1, 3, 2)
    sibling = dev(c_=oc)
    partner = dev(zh_=ozh)
    pairs = (
        (x_hbm, x_ref), (wm_hbm, wm_ref), (brow_hbm, brow_ref), (bcol_hbm, bcol_ref),
        (ws_hbm, ws_ref), (bias_hbm, bias_ref), (wo_hbm, wo_ref), (cot_hbm, cot_ref),
    )
    loads = [pltpu.make_async_copy(a, b, in_sems.at[i]) for i, (a, b) in enumerate(pairs)]
    for copy in loads:
        copy.start()
    partners = [partner, sibling]
    for d in near:
        partners += [dev(zl_=around(zl, d)), dev(y_=around(y, d)), dev(x_=around(x, d))]
    barrier = pltpu.get_barrier_semaphore()
    for p in partners:
        pl.semaphore_signal(barrier, inc=1, device_id=p, device_id_type=MESH)
    load_values = pltpu.make_async_copy(values_ref.at[0], vals, v_sem)
    load_values.start()

    sent = []

    def send(src, dst, recv, to):
        copy = pltpu.make_async_remote_copy(
            src_ref=src, dst_ref=dst, send_sem=send_sems.at[len(sent)], recv_sem=recv,
            device_id=to, device_id_type=MESH,
        )
        copy.start()
        sent.append(copy)

    def share(ref, recv, to):
        send(ref, ref, recv, to)

    def arrived(dst, recv):
        pltpu.make_async_remote_copy(
            src_ref=dst, dst_ref=dst, send_sem=send_sems.at[0], recv_sem=recv,
            device_id=sibling, device_id_type=MESH,
        ).wait_recv()

    def head(c_, zl_, y_):
        return gath.at[c_ * 4 + zl_, y_, pl.ds(0, 3)]

    def tail(c_, zl_, y_):
        return gath.at[c_ * 4 + zl_, y_, 3]

    def tails(c_, zl_):
        return gath.at[c_ * 4 + zl_, :, 3]

    loads[0].wait()
    loads[1].wait()
    feats = x_ref[...]
    gath[c * 4 + zl, y] = dot(feats, wm_ref[...]).astype(BF16).reshape(4, 64, HID)
    xgath[zl, y] = feats
    pl.semaphore_wait(barrier, len(partners))
    for d in near:
        share(head(c, zl, y), p1za.at[zl], dev(zl_=around(zl, d)))
    for d in near:
        share(tail(c, zl, y), p1yb.at[y], dev(y_=around(y, d)))
    for d in near:
        share(head(c, zl, y), p1ya.at[zl, y], dev(y_=around(y, d)))
    share(head(c, zl, y), p1ca.at[zl, y], sibling)

    for copy in loads[2:]:
        copy.wait()
    used = used_ref[0]
    idx_v[...] = jnp.zeros_like(idx_v)
    idx_v[0:1, 0:NBLK] = brow_ref[...]
    idx_v[1:2, 0:NBLK] = bcol_ref[...]
    lane = lax.broadcasted_iota(jnp.int32, (1, NB_PAD), 1)
    lanes = lax.broadcasted_iota(jnp.int32, (NB_PAD, NB_PAD), 1)
    usable = lane < used
    rows_of = idx_v[0:1, :]
    cols_of = idx_v[1:2, :]
    source = cols_of >> 1
    tile_of = (((source & 1) * 16 + (source >> 3) * 4 + ((source >> 1) & 3)) << 1) + (cols_of & 1)

    def listing(key, other):
        packed = (((key << 8) + lane) << 7) + other
        along = jnp.broadcast_to(packed, (NB_PAD, NB_PAD))
        down = along.T
        rank = jnp.sum((along < down).astype(jnp.int32), axis=1, keepdims=True)
        ordered = jnp.sum(jnp.where(rank == lanes, down, 0), axis=0, keepdims=True)
        keys = down >> 15
        upto = jnp.sum((keys <= lanes).astype(jnp.int32), axis=0, keepdims=True)
        below = jnp.sum((keys < lanes).astype(jnp.int32), axis=0, keepdims=True)
        return ordered, jnp.where(upto > below, upto - 1, ZERO_SLOT)

    def list_blocks():
        order_f, end_f = listing(jnp.where(usable, rows_of, BROWS), tile_of)
        order_b, end_b = listing(jnp.where(usable, tile_of, CTILES), rows_of)
        idx_v[0:1, :] = order_f
        idx_v[1:2, :] = end_f
        idx_v[2:3, :] = order_b
        idx_v[3:4, :] = end_b

    list_blocks()
    load_index = pltpu.make_async_copy(idx_v, idx_s, i_sem)
    load_index.start()

    def pass_head(d):
        zs = around(zl, d)
        arrived(head(c, zs, y), p1za.at[zs])
        for e in near:
            share(head(c, zs, y), p1ya.at[zs, y], dev(y_=around(y, e)))
        share(head(c, zs, y), p1ca.at[zs, y], sibling)

    pass_head(1)
    for e in near:
        ys = around(y, e)
        arrived(tail(c, zl, ys), p1yb.at[ys])
    for d in near:
        share(tails(c, zl), p1zb.at[zl], dev(zl_=around(zl, d)))
    share(tails(c, zl), p1cb.at[zl], sibling)
    pass_head(3)
    pass_head(2)

    ident[...] = dot(feats, ws_ref[...]) + bias_ref[...]
    cot = cot_ref[...]
    hgrad[...] = dot(cot, wo_ref[...], ((1,), (1,)))
    runs[ZERO_SLOT] = jnp.zeros((TILE, HID), F32)

    for d in (0,) + near:
        zs = around(zl, d)
        for e in near:
            ys = around(y, e)
            arrived(head(c, zs, ys), p1ya.at[zs, ys])
            share(head(c, zs, ys), p1ca.at[zs, ys], sibling)
        if d:
            arrived(tails(c, zs), p1zb.at[zs])
            share(tails(c, zs), p1cb.at[zs], sibling)
    load_values.wait()
    load_index.wait()
    for zs in range(4):
        arrived(tails(oc, zs), p1cb.at[zs])
        for ys in range(4):
            arrived(head(oc, zs, ys), p1ca.at[zs, ys])

    def pass_raw(steps):
        for d in steps:
            zs = around(zl, d)
            if d:
                arrived(xgath.at[zs, y], xgz.at[zs])
            for e in near:
                share(xgath.at[zs, y], xgy.at[zs, y], dev(y_=around(y, e)))

    for d in near:
        share(xgath.at[zl, y], xgz.at[zl], dev(zl_=around(zl, d)))
    pass_raw((0,))

    def products(which, pick):
        def step(i, carry):
            total, before = carry
            for u in range(UNROLL):
                p = i * UNROLL + u
                word = idx_s[which, p]
                key = word >> 15
                term = pick((word >> 7) & 255, word & 127)
                total = jnp.where(key == before, total, 0.0) + term
                runs[p] = total
                before = key
            return total, before

        lax.fori_loop(0, NBLK // UNROLL, step, (jnp.zeros((TILE, HID), F32), jnp.int32(-1)))

    def source_tile(o):
        a, b, q = o >> 3, (o >> 1) & 3, (o & 1) * 2
        return jnp.concatenate([gath[a, b, q], gath[a, b, q + 1]], axis=0)

    products(0, lambda b, o: dot(vals[b], source_tile(o)))

    def part(j, k):
        return runs[idx_s[1, j * 2 + k]]

    for zz, recv_sems, recv in ((ozh, r3a, recv_a), (zh, r3b, recv_b)):
        for k in range(2):
            for d in near:
                xs = around(x, d)
                j = xs * 2 + zz
                part_send[j, k] = part(j, k).astype(BF16)
                send(part_send.at[j, k], recv.at[x, k], recv_sems.at[x, k], dev(x_=xs))

    def summed(recv, recv_sems, zz, k):
        total = part(x * 2 + zz, k)
        for d in near:
            xs = around(x, d)
            arrived(recv.at[xs, k], recv_sems.at[xs, k])
            total = total + recv[xs, k].astype(F32)
        return total

    for k in range(2):
        zsend[k] = summed(recv_a, r3a, ozh, k).astype(BF16)
        send(zsend.at[k], recv_z.at[k], r3z.at[k], partner)
    pass_raw((1, 3))
    agg = [summed(recv_b, r3b, zh, k) for k in range(2)]
    hidden, pgrad = [], []
    for k in range(2):
        here = pl.ds(k * TILE, TILE)
        arrived(recv_z.at[k], r3z.at[k])
        pre = ident[here, :] + (agg[k] + recv_z[k].astype(F32))
        sig = jax.nn.sigmoid(pre)
        grad = hgrad[here, :] * sig * (1.0 + pre * (1.0 - sig))
        pgt[rep, k] = grad.T.astype(BF16)
        share(pgt.at[rep, k], r5z.at[k], partner)
        for d in near:
            share(pgt.at[rep, k], r5x.at[x, k], dev(x_=around(x, d)))
        hidden.append((pre * sig).astype(BF16))
        pgrad.append(grad.astype(BF16))

    pass_raw((2,))
    hid = jnp.concatenate(hidden, axis=0)
    pg = jnp.concatenate(pgrad, axis=0)
    updated_ref[...] = (feats.astype(F32) + dot(hid, wo_ref[...])).astype(BF16)
    base[...] = cot.astype(F32) + dot(pg, ws_ref[...], ((1,), (1,)))
    term_self = dot(feats, pg, ((0,), (0,)))
    term_out = dot(hid, cot, ((0,), (0,)))
    term_bias = jnp.sum(pg.astype(F32).reshape(32, 8, HID), axis=0)
    for h in range(2):
        m_a[h, :, :, 0:8, :] = term_self[h * 128:(h + 1) * 128, :].reshape(4, 4, 8, HID)
        m_a[h, :, :, 8:16, :] = term_out[:, h * 128:(h + 1) * 128].reshape(4, 4, 8, HID)
        m_a[h, :, :, 16:24, :] = jnp.broadcast_to(term_bias[None, None], (4, 4, 8, HID))
    send(m_a.at[oc], a_core, aa_c.at[0], sibling)

    oj = x * 2 + ozh
    for k in range(2):
        arrived(pgt.at[oj, k], r5z.at[k])
        for d in near:
            share(pgt.at[oj, k], r5f.at[x, k], dev(x_=around(x, d)))
    spot = c * 16 + x * 4 + y
    level = zh * 4 + zl

    def plane():
        for a in (2, 1, 3, 0):
            for b in (2, 1, 3, 0):
                for cc in (1, 0):
                    if (cc, a, b) != (0, 0, 0):
                        ct, xt, yt = (c + cc) % 2, around(x, a), around(y, b)
                        yield ct * 16 + xt * 4 + yt, dev(c_=ct, x_=xt, y_=yt)

    def column_devices():
        for d in (4, 3, 5, 2, 6, 1, 7):
            z = (level + d) % 8
            yield z, dev(zl_=z % 4, zh_=z // 4)

    def grads_scatter(m, m_in, sem):
        m_in[spot] = m[spot]
        for q, to in plane():
            send(m.at[q], m_in.at[spot], sem.at[spot], to)

    def grads_level(m_in, m_rep, sem_in, sem):
        for q, _ in plane():
            arrived(m_in.at[q], sem_in.at[q])
        total = m_in[0]
        for q in range(1, 32):
            total = total + m_in[q]
        m_rep[level] = total
        for _, to in column_devices():
            share(m_rep.at[level], sem.at[level], to)

    def grads_spread(m_rep, m_fin, sem_rep, sem):
        for z, _ in column_devices():
            arrived(m_rep.at[z], sem_rep.at[z])
        total = m_rep[0]
        for z in range(1, 8):
            total = total + m_rep[z]
        m_fin[spot] = total
        for _, to in plane():
            share(m_fin.at[spot], sem.at[spot], to)

    def grads_end(m_fin, sem_out):
        for q, _ in plane():
            arrived(m_fin.at[q], sem_out.at[q])

    def sums_x():
        arrived(a_core, aa_c.at[0])
        a_core[...] = a_core[...] + m_a[c]
        for d in near:
            xs = around(x, d)
            send(a_core.at[xs], a_x.at[x], aa_x.at[x], dev(x_=xs))

    def sums_y():
        total = a_core[x]
        for d in near:
            xs = around(x, d)
            arrived(a_x.at[xs], aa_x.at[xs])
            total = total + a_x[xs]
        a_x[x] = total
        for d in near:
            ys = around(y, d)
            send(a_x.at[x, ys], a_y.at[y], aa_y.at[y], dev(y_=ys))

    def sums_z():
        total = a_x[x, y]
        for d in near:
            ys = around(y, d)
            arrived(a_y.at[ys], aa_y.at[ys])
            total = total + a_y[ys]
        m_a_rep[level] = total
        for _, to in column_devices():
            share(m_a_rep.at[level], aa_z.at[level], to)

    def spread_x():
        for z, _ in column_devices():
            arrived(m_a_rep.at[z], aa_z.at[z])
        total = m_a_rep[0]
        for z in range(1, 8):
            total = total + m_a_rep[z]
        m_a_fin[c, x, y] = total
        for d in near:
            share(m_a_fin.at[c, x, y], aa_ox.at[x], dev(x_=around(x, d)))

    def spread_y():
        for d in near:
            xs = around(x, d)
            arrived(m_a_fin.at[c, xs, y], aa_ox.at[xs])
        for d in near:
            share(m_a_fin.at[c, :, y], aa_oy.at[y], dev(y_=around(y, d)))

    def spread_core():
        for d in near:
            ys = around(y, d)
            arrived(m_a_fin.at[c, :, ys], aa_oy.at[ys])
        share(m_a_fin.at[c], aa_oc.at[0], sibling)

    sums_x()
    for k in range(2):
        for d in near:
            xs = around(x, d)
            arrived(pgt.at[xs * 2 + zh, k], r5x.at[xs, k])
            arrived(pgt.at[xs * 2 + ozh, k], r5f.at[xs, k])
    sums_y()
    products(2, lambda b, o: dot(pgt[o >> 1, o & 1], vals[b]))
    sums_z()

    def column(c_, zl_, y_, k):
        return runs[idx_s[3, ((c_ * 4 + zl_) * 4 + y_) * 2 + k]]

    for d in near + (0,):
        zs = around(zl, d)
        for ys in range(4):
            for k in range(2):
                t_send[zs, ys, k * TILE:(k + 1) * TILE, :] = column(oc, zs, ys, k).astype(BF16)
        send(t_send.at[zs], recv_c.at[zs], r7c.at[zs], sibling)
    def send_heads(zs):
        for e in near:
            ys = around(y, e)
            send(t_sum.at[zs, ys, pl.ds(0, CUT)], recv_ya.at[y, zs], r7ya.at[y, zs], dev(y_=ys))

    for d in near + (0,):
        zs = around(zl, d)
        arrived(recv_c.at[zs], r7c.at[zs])
        for ys in range(4):
            for k in range(2):
                here = slice(k * TILE, (k + 1) * TILE)
                total = column(c, zs, ys, k) + recv_c[zs, ys, here, :].astype(F32)
                t_sum[zs, ys, here, :] = total.astype(BF16)
        if d:
            send(t_sum.at[zs, :, pl.ds(CUT, 256 - CUT)], recv_zb.at[zl], r7zb.at[zl], dev(zl_=zs))
        if d in (1, 3):
            send_heads(zs)

    for e in near:
        ys = around(y, e)
        for zs in range(4):
            arrived(xgath.at[zs, ys], xgy.at[zs, ys])

    def message(zs, total):
        for ys in range(4):
            both = jnp.concatenate([t_sum[zs, ys, 0:TILE, :], t_sum[zs, ys, TILE:256, :]], axis=1)
            total = total + dot(both, xgath[zs, ys])
        return total

    term_msg = lax.fori_loop(0, 4, message, jnp.zeros((HID, FEAT), F32))
    m_b[...] = term_msg.T.reshape(32, 8, HID)
    grads_scatter(m_b, m_b_in, ab_in)
    for d in (2, 0):
        send_heads(around(zl, d))
    spread_x()

    def heads(zs):
        total = t_sum[zs, y, 0:CUT, :].astype(F32)
        for e in near:
            ys = around(y, e)
            arrived(recv_ya.at[ys, zs], r7ya.at[ys, zs])
            total = total + recv_ya[ys, zs].astype(F32)
        return total

    for d in near:
        zs = around(zl, d)
        za_send[zs] = heads(zs).astype(BF16)
        send(za_send.at[zs], recv_za.at[zl], r7za.at[zl], dev(zl_=zs))
    spread_y()
    grads_level(m_b_in, m_b_rep, ab_in, ab_rep)
    for d in near:
        zs = around(zl, d)
        arrived(recv_zb.at[zs], r7zb.at[zs])
    for e in near + (0,):
        ys = around(y, e)
        final_b = t_sum[zl, ys, CUT:256, :].astype(F32)
        for d in near:
            final_b = final_b + recv_zb[around(zl, d), ys].astype(F32)
        if e:
            yb_send[ys] = final_b.astype(BF16)
            send(yb_send.at[ys], recv_yb.at[y], r7yb.at[y], dev(y_=ys))
    spread_core()
    final_a = heads(zl)
    for d in near:
        zs = around(zl, d)
        arrived(recv_za.at[zs], r7za.at[zs])
        final_a = final_a + recv_za[zs].astype(F32)
    for e in near:
        ys = around(y, e)
        arrived(recv_yb.at[ys], r7yb.at[ys])
        final_b = final_b + recv_yb[ys].astype(F32)
    grads_spread(m_b_rep, m_b_fin, ab_rep, ab_out)
    second = jnp.concatenate([final_a[TILE:CUT], final_b], axis=0)
    for k, total in enumerate((final_a[0:TILE], second)):
        here = pl.ds(k * TILE, TILE)
        gnodes_ref[here, :] = (
            base[here, :] + dot(total.T.astype(BF16), wm_ref[...], ((1,), (1,)))
        ).astype(BF16)
    stores = [
        pltpu.make_async_copy(a, b, out_sems.at[i])
        for i, (a, b) in enumerate((
            (updated_ref, updated_hbm), (gnodes_ref, gnodes_hbm), (gself_ref, gself_hbm),
            (gout_ref, gout_hbm), (gbias_ref, gbias_hbm), (gmsg_ref, gmsg_hbm),
        ))
    ]
    stores[0].start()
    stores[1].start()
    arrived(m_a_fin.at[oc], aa_oc.at[0])
    factor = 1.0 / math.sqrt(65536)
    for h in range(2):
        half = slice(h * 128, (h + 1) * 128)
        gself_ref[half, :] = m_a_fin[h, :, :, 0:8, :].reshape(128, HID) * factor
        gout_ref[:, half] = m_a_fin[h, :, :, 8:16, :].reshape(HID, 128) * factor
    gbias_ref[...] = jnp.sum(m_a_fin[0, 0, 0, 16:24, :], axis=0, keepdims=True) * factor
    for copy in stores[2:5]:
        copy.start()
    grads_end(m_b_fin, ab_out)
    gmsg_ref[...] = m_b_fin[...].reshape(FEAT, HID) * factor
    stores[5].start()
    for copy in sent:
        copy.wait_send()
    for copy in stores:
        copy.wait()


def write_out(*refs):
    ins, outs, held, sems = refs[:6], refs[6:12], refs[12:18], refs[18]
    loads = [pltpu.make_async_copy(ins[i], held[i], sems.at[0, i]) for i in range(6)]
    stores = [pltpu.make_async_copy(held[i], outs[i], sems.at[1, i]) for i in range(6)]
    for copy in loads:
        copy.start()
    for load, store in zip(loads, stores):
        load.wait()
        store.start()
    for copy in stores:
        copy.wait()


def body(x, values, brow, bcol, used, ws, wm, bias, wo, cot):
    dma = pltpu.SemaphoreType.DMA

    out_shape = (
        jax.ShapeDtypeStruct((256, FEAT), BF16),
        jax.ShapeDtypeStruct((256, FEAT), BF16),
        jax.ShapeDtypeStruct((FEAT, HID), F32),
        jax.ShapeDtypeStruct((FEAT, HID), F32),
        jax.ShapeDtypeStruct((HID, FEAT), F32),
        jax.ShapeDtypeStruct((1, HID), F32),
    )
    hbm = pl.BlockSpec(memory_space=pltpu.HBM)
    results = pl.pallas_call(
        kernel,
        out_shape=out_shape,
        in_specs=[pl.BlockSpec(memory_space=pltpu.SMEM)] + [hbm] * 9,
        out_specs=(hbm,) * 6,
        scratch_shapes=[
            *[pltpu.VMEM(shape.shape, shape.dtype) for shape in out_shape],
            pltpu.VMEM((256, FEAT), BF16),
            pltpu.VMEM((1, NBLK), jnp.int32),
            pltpu.VMEM((1, NBLK), jnp.int32),
            pltpu.VMEM((FEAT, HID), BF16),
            pltpu.VMEM((FEAT, HID), BF16),
            pltpu.VMEM((1, HID), F32),
            pltpu.VMEM((HID, FEAT), BF16),
            pltpu.VMEM((256, FEAT), BF16),
            pltpu.VMEM((NBLK, TILE, TILE), BF16),
            pltpu.VMEM((8, 4, 4, 64, HID), BF16),
            pltpu.VMEM((4, 4, 256, FEAT), BF16),
            pltpu.VMEM((NBLK + 1, TILE, HID), F32),
            pltpu.VMEM((8, NB_PAD), jnp.int32),
            pltpu.SMEM((8, NB_PAD), jnp.int32),
            pltpu.VMEM((256, HID), F32),
            pltpu.VMEM((256, FEAT), F32),
            pltpu.VMEM((256, HID), F32),
            pltpu.VMEM((8, 2, TILE, HID), BF16),
            pltpu.VMEM((4, 2, TILE, HID), BF16),
            pltpu.VMEM((4, 2, TILE, HID), BF16),
            pltpu.VMEM((2, TILE, HID), BF16),
            pltpu.VMEM((2, TILE, HID), BF16),
            pltpu.VMEM((8, 2, HID, TILE), BF16),
            pltpu.VMEM((4, 4, 256, TILE), BF16),
            pltpu.VMEM((4, 4, 256, TILE), BF16),
            pltpu.VMEM((4, 4, 256, TILE), BF16),
            pltpu.VMEM((4, 4, CUT, TILE), BF16),
            pltpu.VMEM((4, CUT, TILE), BF16),
            pltpu.VMEM((4, CUT, TILE), BF16),
            pltpu.VMEM((4, 4, 256 - CUT, TILE), BF16),
            pltpu.VMEM((4, 256 - CUT, TILE), BF16),
            pltpu.VMEM((4, 256 - CUT, TILE), BF16),
            *[pltpu.VMEM((*lead, 24, HID), F32) for lead in ((2, 4, 4), (4, 4), (4,), (4, 4), (8,), (2, 4, 4))],
            *[pltpu.VMEM((lead, 8, HID), F32) for lead in (32, 32, 8, 32)],
            dma((8,)), dma((6,)), dma, dma, dma((280,)),
            dma((4,)), dma((4, 4)), dma((4,)), dma((4,)), dma((4, 4)), dma((4,)), dma((4,)), dma((4, 4)),
            dma((4, 2)), dma((4, 2)), dma((2,)), dma((4, 2)), dma((2,)), dma((4, 2)),
            dma((4,)), dma((4, 4)), dma((4,)), dma((4,)), dma((4,)),
            dma((1,)), dma((4,)), dma((4,)), dma((8,)), dma((4,)), dma((4,)), dma((1,)),
            dma((32,)), dma((8,)), dma((32,)),
        ],
        compiler_params=pltpu.CompilerParams(
            collective_id=0, has_side_effects=True, vmem_limit_bytes=63 * 2**20
        ),
        name="layer",
    )(used, x, values, brow, bcol, ws, wm, bias.reshape(1, HID), wo, cot)
    updated, gnodes, gself, gmsg, gout, gbias = pl.pallas_call(
        write_out,
        out_shape=out_shape,
        in_specs=[hbm] * 6,
        out_specs=(hbm,) * 6,
        scratch_shapes=[*[pltpu.VMEM(shape.shape, shape.dtype) for shape in out_shape], dma((2, 6))],
        name="write_out",
    )(*results)
    return updated, gnodes, gself, gmsg, gout, gbias.reshape(HID)


def solution(mesh):
    sharded = P(("rows", "rep"), None)
    in_specs = (
        sharded, P(("rows", "rep"), None, None, None), sharded, sharded, P(("rows", "rep")),
        P(), P(), P(), P(), sharded,
    )
    out_specs = (sharded, sharded, P(), P(), P(), P())
    return jax.shard_map(body, mesh=mesh, in_specs=in_specs, out_specs=out_specs, check_vma=False)
```

```python
import functools
import math

import jax
import jax.numpy as jnp
from jax import lax
from jax.experimental import pallas as pl
from jax.experimental.pallas import tpu as pltpu
from jax.sharding import PartitionSpec as P

FEAT = 256
HID = 128
TILE = 128
NBLK = 176
NB_PAD = 256
BROWS = 16
CTILES = 64
ZERO_SLOT = NBLK
MESH = pl.DeviceIdType.MESH
F32 = jnp.float32
BF16 = jnp.bfloat16
UNROLL = 44
CUT = 192


def dot(a, b, dims=((1,), (0,))):
    return lax.dot_general(a, b, (dims, ((), ())), preferred_element_type=F32)


def kernel(
    used_ref, x_hbm, values_ref, brow_hbm, bcol_hbm, ws_hbm, wm_hbm, bias_hbm, wo_hbm, cot_hbm,
    updated_hbm, gnodes_hbm, gself_hbm, gmsg_hbm, gout_hbm, gbias_hbm,
    updated_ref, gnodes_ref, gself_ref, gmsg_ref, gout_ref, gbias_ref,
    x_ref, brow_ref, bcol_ref, ws_ref, wm_ref, bias_ref, wo_ref, cot_ref,
    vals, gath, xgath, runs, idx_v, idx_s, ident, base, hgrad,
    part_send, recv_a, recv_b, zsend, recv_z, pgt,
    t_send, recv_c, t_sum, recv_ya, za_send, recv_za, recv_zb, yb_send, recv_yb,
    m_a, a_core, a_y, a_x, m_a_rep, m_a_fin, m_b, m_b_in, m_b_rep, m_b_fin,
    in_sems, out_sems, v_sem, i_sem, send_sems,
    p1za, p1ya, p1yb, p1zb, p1ca, p1cb, xgz, xgy,
    r3a, r3b, r3z, r5x, r5z, r5f, r7c, r7ya, r7za, r7zb, r7yb,
    aa_c, aa_y, aa_x, aa_z, aa_ox, aa_oy, aa_oc, ab_in, ab_rep, ab_out,
):
    row = lax.axis_index("rows")
    rep = lax.axis_index("rep")
    zl, y, c = row // 8, (row // 2) % 4, row % 2
    x, zh = rep // 2, rep % 2
    oc, ozh = 1 - c, 1 - zh

    def dev(zl_=None, y_=None, c_=None, x_=None, zh_=None):
        zl_ = zl if zl_ is None else zl_
        y_ = y if y_ is None else y_
        c_ = c if c_ is None else c_
        x_ = x if x_ is None else x_
        zh_ = zh if zh_ is None else zh_
        return {"rows": zl_ * 8 + y_ * 2 + c_, "rep": x_ * 2 + zh_}

    def around(i, d):
        return (i + d) % 4

    near = (1, 3, 2)
    sibling = dev(c_=oc)
    partner = dev(zh_=ozh)
    pairs = (
        (x_hbm, x_ref), (wm_hbm, wm_ref), (brow_hbm, brow_ref), (bcol_hbm, bcol_ref),
        (ws_hbm, ws_ref), (bias_hbm, bias_ref), (wo_hbm, wo_ref), (cot_hbm, cot_ref),
    )
    loads = [pltpu.make_async_copy(a, b, in_sems.at[i]) for i, (a, b) in enumerate(pairs)]
    for copy in loads:
        copy.start()
    partners = [partner, sibling]
    for d in near:
        partners += [dev(zl_=around(zl, d)), dev(y_=around(y, d)), dev(x_=around(x, d))]
    barrier = pltpu.get_barrier_semaphore()
    for p in partners:
        pl.semaphore_signal(barrier, inc=1, device_id=p, device_id_type=MESH)
    load_values = pltpu.make_async_copy(values_ref.at[0], vals, v_sem)
    load_values.start()

    sent = []

    def send(src, dst, recv, to):
        copy = pltpu.make_async_remote_copy(
            src_ref=src, dst_ref=dst, send_sem=send_sems.at[len(sent)], recv_sem=recv,
            device_id=to, device_id_type=MESH,
        )
        copy.start()
        sent.append(copy)

    def share(ref, recv, to):
        send(ref, ref, recv, to)

    def arrived(dst, recv):
        pltpu.make_async_remote_copy(
            src_ref=dst, dst_ref=dst, send_sem=send_sems.at[0], recv_sem=recv,
            device_id=sibling, device_id_type=MESH,
        ).wait_recv()

    def head(c_, zl_, y_):
        return gath.at[c_ * 4 + zl_, y_, pl.ds(0, 3)]

    def tail(c_, zl_, y_):
        return gath.at[c_ * 4 + zl_, y_, 3]

    def tails(c_, zl_):
        return gath.at[c_ * 4 + zl_, :, 3]

    loads[0].wait()
    loads[1].wait()
    feats = x_ref[...]
    gath[c * 4 + zl, y] = dot(feats, wm_ref[...]).astype(BF16).reshape(4, 64, HID)
    xgath[zl, y] = feats
    pl.semaphore_wait(barrier, len(partners))
    for d in near:
        share(head(c, zl, y), p1za.at[zl], dev(zl_=around(zl, d)))
    for d in near:
        share(tail(c, zl, y), p1yb.at[y], dev(y_=around(y, d)))
    for d in near:
        share(head(c, zl, y), p1ya.at[zl, y], dev(y_=around(y, d)))
    share(head(c, zl, y), p1ca.at[zl, y], sibling)

    for copy in loads[2:]:
        copy.wait()
    used = used_ref[0]
    idx_v[...] = jnp.zeros_like(idx_v)
    idx_v[0:1, 0:NBLK] = brow_ref[...]
    idx_v[1:2, 0:NBLK] = bcol_ref[...]
    lane = lax.broadcasted_iota(jnp.int32, (1, NB_PAD), 1)
    lanes = lax.broadcasted_iota(jnp.int32, (NB_PAD, NB_PAD), 1)
    usable = lane < used
    rows_of = idx_v[0:1, :]
    cols_of = idx_v[1:2, :]
    source = cols_of >> 1
    tile_of = (((source & 1) * 16 + (source >> 3) * 4 + ((source >> 1) & 3)) << 1) + (cols_of & 1)

    def listing(key, other):
        packed = (((key << 8) + lane) << 7) + other
        along = jnp.broadcast_to(packed, (NB_PAD, NB_PAD))
        down = along.T
        rank = jnp.sum((along < down).astype(jnp.int32), axis=1, keepdims=True)
        ordered = jnp.sum(jnp.where(rank == lanes, down, 0), axis=0, keepdims=True)
        keys = down >> 15
        upto = jnp.sum((keys <= lanes).astype(jnp.int32), axis=0, keepdims=True)
        below = jnp.sum((keys < lanes).astype(jnp.int32), axis=0, keepdims=True)
        return ordered, jnp.where(upto > below, upto - 1, ZERO_SLOT)

    def list_blocks():
        order_f, end_f = listing(jnp.where(usable, rows_of, BROWS), tile_of)
        order_b, end_b = listing(jnp.where(usable, tile_of, CTILES), rows_of)
        idx_v[0:1, :] = order_f
        idx_v[1:2, :] = end_f
        idx_v[2:3, :] = order_b
        idx_v[3:4, :] = end_b

    list_blocks()
    load_index = pltpu.make_async_copy(idx_v, idx_s, i_sem)
    load_index.start()

    def pass_head(d):
        zs = around(zl, d)
        arrived(head(c, zs, y), p1za.at[zs])
        for e in near:
            share(head(c, zs, y), p1ya.at[zs, y], dev(y_=around(y, e)))
        share(head(c, zs, y), p1ca.at[zs, y], sibling)

    pass_head(1)
    for e in near:
        ys = around(y, e)
        arrived(tail(c, zl, ys), p1yb.at[ys])
    for d in near:
        share(tails(c, zl), p1zb.at[zl], dev(zl_=around(zl, d)))
    share(tails(c, zl), p1cb.at[zl], sibling)
    pass_head(3)
    pass_head(2)

    ident[...] = dot(feats, ws_ref[...]) + bias_ref[...]
    cot = cot_ref[...]
    hgrad[...] = dot(cot, wo_ref[...], ((1,), (1,)))
    runs[ZERO_SLOT] = jnp.zeros((TILE, HID), F32)

    for d in (0,) + near:
        zs = around(zl, d)
        for e in near:
            ys = around(y, e)
            arrived(head(c, zs, ys), p1ya.at[zs, ys])
            share(head(c, zs, ys), p1ca.at[zs, ys], sibling)
        if d:
            arrived(tails(c, zs), p1zb.at[zs])
            share(tails(c, zs), p1cb.at[zs], sibling)
    load_values.wait()
    load_index.wait()
    for zs in range(4):
        arrived(tails(oc, zs), p1cb.at[zs])
        for ys in range(4):
            arrived(head(oc, zs, ys), p1ca.at[zs, ys])

    def pass_raw(steps):
        for d in steps:
            zs = around(zl, d)
            if d:
                arrived(xgath.at[zs, y], xgz.at[zs])
            for e in near:
                share(xgath.at[zs, y], xgy.at[zs, y], dev(y_=around(y, e)))

    for d in near:
        share(xgath.at[zl, y], xgz.at[zl], dev(zl_=around(zl, d)))
    pass_raw((0,))

    def products(which, pick):
        def step(i, carry):
            total, before = carry
            for u in range(UNROLL):
                p = i * UNROLL + u
                word = idx_s[which, p]
                key = word >> 15
                term = pick((word >> 7) & 255, word & 127)
                total = jnp.where(key == before, total, 0.0) + term
                runs[p] = total
                before = key
            return total, before

        lax.fori_loop(0, NBLK // UNROLL, step, (jnp.zeros((TILE, HID), F32), jnp.int32(-1)))

    def source_tile(o):
        a, b, q = o >> 3, (o >> 1) & 3, (o & 1) * 2
        return jnp.concatenate([gath[a, b, q], gath[a, b, q + 1]], axis=0)

    products(0, lambda b, o: dot(vals[b], source_tile(o)))

    def part(j, k):
        return runs[idx_s[1, j * 2 + k]]

    for zz, recv_sems, recv in ((ozh, r3a, recv_a), (zh, r3b, recv_b)):
        for k in range(2):
            for d in near:
                xs = around(x, d)
                j = xs * 2 + zz
                part_send[j, k] = part(j, k).astype(BF16)
                send(part_send.at[j, k], recv.at[x, k], recv_sems.at[x, k], dev(x_=xs))

    def summed(recv, recv_sems, zz, k):
        total = part(x * 2 + zz, k)
        for d in near:
            xs = around(x, d)
            arrived(recv.at[xs, k], recv_sems.at[xs, k])
            total = total + recv[xs, k].astype(F32)
        return total

    for k in range(2):
        zsend[k] = summed(recv_a, r3a, ozh, k).astype(BF16)
        send(zsend.at[k], recv_z.at[k], r3z.at[k], partner)
    pass_raw((1, 3))
    agg = [summed(recv_b, r3b, zh, k) for k in range(2)]
    hidden, pgrad = [], []
    for k in range(2):
        here = pl.ds(k * TILE, TILE)
        arrived(recv_z.at[k], r3z.at[k])
        pre = ident[here, :] + (agg[k] + recv_z[k].astype(F32))
        sig = jax.nn.sigmoid(pre)
        grad = hgrad[here, :] * sig * (1.0 + pre * (1.0 - sig))
        pgt[rep, k] = grad.T.astype(BF16)
        share(pgt.at[rep, k], r5z.at[k], partner)
        for d in near:
            share(pgt.at[rep, k], r5x.at[x, k], dev(x_=around(x, d)))
        hidden.append((pre * sig).astype(BF16))
        pgrad.append(grad.astype(BF16))

    pass_raw((2,))
    hid = jnp.concatenate(hidden, axis=0)
    pg = jnp.concatenate(pgrad, axis=0)
    updated_ref[...] = (feats.astype(F32) + dot(hid, wo_ref[...])).astype(BF16)
    base[...] = cot.astype(F32) + dot(pg, ws_ref[...], ((1,), (1,)))
    term_self = dot(feats, pg, ((0,), (0,)))
    term_out = dot(hid, cot, ((0,), (0,)))
    term_bias = jnp.sum(pg.astype(F32).reshape(32, 8, HID), axis=0)
    for h in range(2):
        m_a[h, :, :, 0:8, :] = term_self[h * 128:(h + 1) * 128, :].reshape(4, 4, 8, HID)
        m_a[h, :, :, 8:16, :] = term_out[:, h * 128:(h + 1) * 128].reshape(4, 4, 8, HID)
        m_a[h, :, :, 16:24, :] = jnp.broadcast_to(term_bias[None, None], (4, 4, 8, HID))
    send(m_a.at[oc], a_core, aa_c.at[0], sibling)

    oj = x * 2 + ozh
    for k in range(2):
        arrived(pgt.at[oj, k], r5z.at[k])
        for d in near:
            share(pgt.at[oj, k], r5f.at[x, k], dev(x_=around(x, d)))
    spot = c * 16 + x * 4 + y
    level = zh * 4 + zl

    def plane():
        for a in (2, 1, 3, 0):
            for b in (2, 1, 3, 0):
                for cc in (1, 0):
                    if (cc, a, b) != (0, 0, 0):
                        ct, xt, yt = (c + cc) % 2, around(x, a), around(y, b)
                        yield ct * 16 + xt * 4 + yt, dev(c_=ct, x_=xt, y_=yt)

    def column_devices():
        for d in (4, 3, 5, 2, 6, 1, 7):
            z = (level + d) % 8
            yield z, dev(zl_=z % 4, zh_=z // 4)

    def grads_scatter(m, m_in, sem):
        m_in[spot] = m[spot]
        for q, to in plane():
            send(m.at[q], m_in.at[spot], sem.at[spot], to)

    def grads_level(m_in, m_rep, sem_in, sem):
        for q, _ in plane():
            arrived(m_in.at[q], sem_in.at[q])
        total = m_in[0]
        for q in range(1, 32):
            total = total + m_in[q]
        m_rep[level] = total
        for _, to in column_devices():
            share(m_rep.at[level], sem.at[level], to)

    def grads_spread(m_rep, m_fin, sem_rep, sem):
        for z, _ in column_devices():
            arrived(m_rep.at[z], sem_rep.at[z])
        total = m_rep[0]
        for z in range(1, 8):
            total = total + m_rep[z]
        m_fin[spot] = total
        for _, to in plane():
            share(m_fin.at[spot], sem.at[spot], to)

    def grads_end(m_fin, sem_out):
        for q, _ in plane():
            arrived(m_fin.at[q], sem_out.at[q])

    def sums_x():
        arrived(a_core, aa_c.at[0])
        a_core[...] = a_core[...] + m_a[c]
        for d in near:
            xs = around(x, d)
            send(a_core.at[xs], a_x.at[x], aa_x.at[x], dev(x_=xs))

    def sums_y():
        total = a_core[x]
        for d in near:
            xs = around(x, d)
            arrived(a_x.at[xs], aa_x.at[xs])
            total = total + a_x[xs]
        a_x[x] = total
        for d in near:
            ys = around(y, d)
            send(a_x.at[x, ys], a_y.at[y], aa_y.at[y], dev(y_=ys))

    def sums_z():
        total = a_x[x, y]
        for d in near:
            ys = around(y, d)
            arrived(a_y.at[ys], aa_y.at[ys])
            total = total + a_y[ys]
        m_a_rep[level] = total
        for _, to in column_devices():
            share(m_a_rep.at[level], aa_z.at[level], to)

    def spread_x():
        for z, _ in column_devices():
            arrived(m_a_rep.at[z], aa_z.at[z])
        total = m_a_rep[0]
        for z in range(1, 8):
            total = total + m_a_rep[z]
        m_a_fin[c, x, y] = total
        for d in near:
            share(m_a_fin.at[c, x, y], aa_ox.at[x], dev(x_=around(x, d)))

    def spread_y():
        for d in near:
            xs = around(x, d)
            arrived(m_a_fin.at[c, xs, y], aa_ox.at[xs])
        for d in near:
            share(m_a_fin.at[c, :, y], aa_oy.at[y], dev(y_=around(y, d)))

    def spread_core():
        for d in near:
            ys = around(y, d)
            arrived(m_a_fin.at[c, :, ys], aa_oy.at[ys])
        share(m_a_fin.at[c], aa_oc.at[0], sibling)

    sums_x()
    for k in range(2):
        for d in near:
            xs = around(x, d)
            arrived(pgt.at[xs * 2 + zh, k], r5x.at[xs, k])
            arrived(pgt.at[xs * 2 + ozh, k], r5f.at[xs, k])
    sums_y()
    products(2, lambda b, o: dot(pgt[o >> 1, o & 1], vals[b]))
    sums_z()

    def column(c_, zl_, y_, k):
        return runs[idx_s[3, ((c_ * 4 + zl_) * 4 + y_) * 2 + k]]

    for d in near + (0,):
        zs = around(zl, d)
        for ys in range(4):
            for k in range(2):
                t_send[zs, ys, k * TILE:(k + 1) * TILE, :] = column(oc, zs, ys, k).astype(BF16)
        send(t_send.at[zs], recv_c.at[zs], r7c.at[zs], sibling)
    def send_heads(zs):
        for e in near:
            ys = around(y, e)
            send(t_sum.at[zs, ys, pl.ds(0, CUT)], recv_ya.at[y, zs], r7ya.at[y, zs], dev(y_=ys))

    term_msg = jnp.zeros((HID, FEAT), F32)
    for d in near + (0,):
        zs = around(zl, d)
        arrived(recv_c.at[zs], r7c.at[zs])
        for ys in range(4):
            for k in range(2):
                here = slice(k * TILE, (k + 1) * TILE)
                total = column(c, zs, ys, k) + recv_c[zs, ys, here, :].astype(F32)
                t_sum[zs, ys, here, :] = total.astype(BF16)
        if d:
            send(t_sum.at[zs, :, pl.ds(CUT, 256 - CUT)], recv_zb.at[zl], r7zb.at[zl], dev(zl_=zs))
        if d in (1, 3):
            send_heads(zs)
        for e in near:
            ys = around(y, e)
            arrived(xgath.at[zs, ys], xgy.at[zs, ys])
        for ys in range(4):
            both = jnp.concatenate([t_sum[zs, ys, 0:TILE, :], t_sum[zs, ys, TILE:256, :]], axis=1)
            term_msg = term_msg + dot(both, xgath[zs, ys])


    m_b[...] = term_msg.T.reshape(32, 8, HID)
    grads_scatter(m_b, m_b_in, ab_in)
    for d in (2, 0):
        send_heads(around(zl, d))
    spread_x()

    def heads(zs):
        total = t_sum[zs, y, 0:CUT, :].astype(F32)
        for e in near:
            ys = around(y, e)
            arrived(recv_ya.at[ys, zs], r7ya.at[ys, zs])
            total = total + recv_ya[ys, zs].astype(F32)
        return total

    for d in near:
        zs = around(zl, d)
        za_send[zs] = heads(zs).astype(BF16)
        send(za_send.at[zs], recv_za.at[zl], r7za.at[zl], dev(zl_=zs))
    spread_y()
    grads_level(m_b_in, m_b_rep, ab_in, ab_rep)
    for d in near:
        zs = around(zl, d)
        arrived(recv_zb.at[zs], r7zb.at[zs])
    for e in near + (0,):
        ys = around(y, e)
        final_b = t_sum[zl, ys, CUT:256, :].astype(F32)
        for d in near:
            final_b = final_b + recv_zb[around(zl, d), ys].astype(F32)
        if e:
            yb_send[ys] = final_b.astype(BF16)
            send(yb_send.at[ys], recv_yb.at[y], r7yb.at[y], dev(y_=ys))
    spread_core()
    final_a = heads(zl)
    for d in near:
        zs = around(zl, d)
        arrived(recv_za.at[zs], r7za.at[zs])
        final_a = final_a + recv_za[zs].astype(F32)
    for e in near:
        ys = around(y, e)
        arrived(recv_yb.at[ys], r7yb.at[ys])
        final_b = final_b + recv_yb[ys].astype(F32)
    grads_spread(m_b_rep, m_b_fin, ab_rep, ab_out)
    second = jnp.concatenate([final_a[TILE:CUT], final_b], axis=0)
    for k, total in enumerate((final_a[0:TILE], second)):
        here = pl.ds(k * TILE, TILE)
        gnodes_ref[here, :] = (
            base[here, :] + dot(total.T.astype(BF16), wm_ref[...], ((1,), (1,)))
        ).astype(BF16)
    stores = [
        pltpu.make_async_copy(a, b, out_sems.at[i])
        for i, (a, b) in enumerate((
            (updated_ref, updated_hbm), (gnodes_ref, gnodes_hbm), (gself_ref, gself_hbm),
            (gout_ref, gout_hbm), (gbias_ref, gbias_hbm), (gmsg_ref, gmsg_hbm),
        ))
    ]
    stores[0].start()
    stores[1].start()
    arrived(m_a_fin.at[oc], aa_oc.at[0])
    factor = 1.0 / math.sqrt(65536)
    for h in range(2):
        half = slice(h * 128, (h + 1) * 128)
        gself_ref[half, :] = m_a_fin[h, :, :, 0:8, :].reshape(128, HID) * factor
        gout_ref[:, half] = m_a_fin[h, :, :, 8:16, :].reshape(HID, 128) * factor
    gbias_ref[...] = jnp.sum(m_a_fin[0, 0, 0, 16:24, :], axis=0, keepdims=True) * factor
    for copy in stores[2:5]:
        copy.start()
    grads_end(m_b_fin, ab_out)
    gmsg_ref[...] = m_b_fin[...].reshape(FEAT, HID) * factor
    stores[5].start()
    for copy in sent:
        copy.wait_send()
    for copy in stores:
        copy.wait()


def write_out(*refs):
    ins, outs, held, sems = refs[:6], refs[6:12], refs[12:18], refs[18]
    loads = [pltpu.make_async_copy(ins[i], held[i], sems.at[0, i]) for i in range(6)]
    stores = [pltpu.make_async_copy(held[i], outs[i], sems.at[1, i]) for i in range(6)]
    for copy in loads:
        copy.start()
    for load, store in zip(loads, stores):
        load.wait()
        store.start()
    for copy in stores:
        copy.wait()


def body(x, values, brow, bcol, used, ws, wm, bias, wo, cot):
    dma = pltpu.SemaphoreType.DMA

    out_shape = (
        jax.ShapeDtypeStruct((256, FEAT), BF16),
        jax.ShapeDtypeStruct((256, FEAT), BF16),
        jax.ShapeDtypeStruct((FEAT, HID), F32),
        jax.ShapeDtypeStruct((FEAT, HID), F32),
        jax.ShapeDtypeStruct((HID, FEAT), F32),
        jax.ShapeDtypeStruct((1, HID), F32),
    )
    hbm = pl.BlockSpec(memory_space=pltpu.HBM)
    results = pl.pallas_call(
        kernel,
        out_shape=out_shape,
        in_specs=[pl.BlockSpec(memory_space=pltpu.SMEM)] + [hbm] * 9,
        out_specs=(hbm,) * 6,
        scratch_shapes=[
            *[pltpu.VMEM(shape.shape, shape.dtype) for shape in out_shape],
            pltpu.VMEM((256, FEAT), BF16),
            pltpu.VMEM((1, NBLK), jnp.int32),
            pltpu.VMEM((1, NBLK), jnp.int32),
            pltpu.VMEM((FEAT, HID), BF16),
            pltpu.VMEM((FEAT, HID), BF16),
            pltpu.VMEM((1, HID), F32),
            pltpu.VMEM((HID, FEAT), BF16),
            pltpu.VMEM((256, FEAT), BF16),
            pltpu.VMEM((NBLK, TILE, TILE), BF16),
            pltpu.VMEM((8, 4, 4, 64, HID), BF16),
            pltpu.VMEM((4, 4, 256, FEAT), BF16),
            pltpu.VMEM((NBLK + 1, TILE, HID), F32),
            pltpu.VMEM((8, NB_PAD), jnp.int32),
            pltpu.SMEM((8, NB_PAD), jnp.int32),
            pltpu.VMEM((256, HID), F32),
            pltpu.VMEM((256, FEAT), F32),
            pltpu.VMEM((256, HID), F32),
            pltpu.VMEM((8, 2, TILE, HID), BF16),
            pltpu.VMEM((4, 2, TILE, HID), BF16),
            pltpu.VMEM((4, 2, TILE, HID), BF16),
            pltpu.VMEM((2, TILE, HID), BF16),
            pltpu.VMEM((2, TILE, HID), BF16),
            pltpu.VMEM((8, 2, HID, TILE), BF16),
            pltpu.VMEM((4, 4, 256, TILE), BF16),
            pltpu.VMEM((4, 4, 256, TILE), BF16),
            pltpu.VMEM((4, 4, 256, TILE), BF16),
            pltpu.VMEM((4, 4, CUT, TILE), BF16),
            pltpu.VMEM((4, CUT, TILE), BF16),
            pltpu.VMEM((4, CUT, TILE), BF16),
            pltpu.VMEM((4, 4, 256 - CUT, TILE), BF16),
            pltpu.VMEM((4, 256 - CUT, TILE), BF16),
            pltpu.VMEM((4, 256 - CUT, TILE), BF16),
            *[pltpu.VMEM((*lead, 24, HID), F32) for lead in ((2, 4, 4), (4, 4), (4,), (4, 4), (8,), (2, 4, 4))],
            *[pltpu.VMEM((lead, 8, HID), F32) for lead in (32, 32, 8, 32)],
            dma((8,)), dma((6,)), dma, dma, dma((280,)),
            dma((4,)), dma((4, 4)), dma((4,)), dma((4,)), dma((4, 4)), dma((4,)), dma((4,)), dma((4, 4)),
            dma((4, 2)), dma((4, 2)), dma((2,)), dma((4, 2)), dma((2,)), dma((4, 2)),
            dma((4,)), dma((4, 4)), dma((4,)), dma((4,)), dma((4,)),
            dma((1,)), dma((4,)), dma((4,)), dma((8,)), dma((4,)), dma((4,)), dma((1,)),
            dma((32,)), dma((8,)), dma((32,)),
        ],
        compiler_params=pltpu.CompilerParams(
            collective_id=0, has_side_effects=True, vmem_limit_bytes=63 * 2**20
        ),
        name="layer",
    )(used, x, values, brow, bcol, ws, wm, bias.reshape(1, HID), wo, cot)
    updated, gnodes, gself, gmsg, gout, gbias = pl.pallas_call(
        write_out,
        out_shape=out_shape,
        in_specs=[hbm] * 6,
        out_specs=(hbm,) * 6,
        scratch_shapes=[*[pltpu.VMEM(shape.shape, shape.dtype) for shape in out_shape], dma((2, 6))],
        name="write_out",
    )(*results)
    return updated, gnodes, gself, gmsg, gout, gbias.reshape(HID)


def solution(mesh):
    sharded = P(("rows", "rep"), None)
    in_specs = (
        sharded, P(("rows", "rep"), None, None, None), sharded, sharded, P(("rows", "rep")),
        P(), P(), P(), P(), sharded,
    )
    out_specs = (sharded, sharded, P(), P(), P(), P())
    return jax.shard_map(body, mesh=mesh, in_specs=in_specs, out_specs=out_specs, check_vma=False)
```
